512 devices in a mesh: noise: 16 (over z_hi, x, core), dp: 32 (over z_lo, y).
Axes of the slice: x: 4, y: 4, z: 16 (z_hi: 2, z_lo: 8; z = z_hi * 8 + z_lo), core: 2. Of those that a mesh axis runs over, the one named last changes fastest.
Arguments:
- noise: bfloat16 [1024, 16384], P('noise', 'dp'), may hold values from -6 to 6
- data: bfloat16 [8192, 16384], P('dp', 'noise'), may hold values from -6 to 6
- timestep: int32 [1024], P('noise'), may hold values from 0 to 999
Outputs:
- inputs_t: bfloat16 [1024, 16384], P('noise', 'dp')
- velocity: bfloat16 [1024, 16384], P('noise', 'dp')
The draws below stay inside these ranges and needn't reach their ends.
All inputs are finite; a program needn't handle non-finite values.
Results may differ from the reference program's by a relative error of at most 0.011.
Values may be sent and summed in bfloat16 or wider, within the bound.
A program may use at most 64 MiB of HBM per device.

```python
import jax
import jax.numpy as jnp

DL = 16384
ITERS = 4
NBINS = 1000
NN = 1024
ND = 8192


def set_ends(array, rng, low, largest):
    extent = array.shape
    spot = [jax.random.randint(jax.random.fold_in(rng, axis), (), 0, extent[axis]) for axis in range(len(extent))]
    array = array.at[tuple(spot)].set(low)
    longest = extent.index(max(extent))
    spot[longest] = (spot[longest] + 1) % extent[longest]
    return array.at[tuple(spot)].set(largest)


def levels(own_key, dims, cuts, least, top_value):
    gain, own = 1.0, jax.random.fold_in(own_key, 6)
    for position, blocks in cuts:
        draws = jnp.exp(jax.random.uniform(jax.random.fold_in(own, position), (blocks,), jnp.float32, least / len(cuts), top_value / len(cuts)))
        gain = gain * jnp.repeat(draws, dims[position] // blocks).reshape([-1 if axis == position else 1 for axis in range(len(dims))])
    return gain


def gaussian(key, shape, deviation, bound, pieces=(), dtype=jnp.bfloat16):
    drawn = jax.random.normal(key, shape, jnp.float32) * deviation
    if len(pieces) > 0:
        drawn = levels(key, shape, pieces, -0.22, 0.18) * drawn
    return jnp.clip(drawn, min=-bound, max=bound).astype(dtype)


def setup_inputs(seed: int = 0) -> dict:
    key_list = jax.random.split(jax.random.key(seed), 4)
    noise = gaussian(key_list[0], (NN, DL), 1.0, 6.0, ((0, 16), (1, 32)))
    data = gaussian(key_list[1], (ND, DL), 1.0, 6.0, ((0, 32), (1, 16)))
    timestep = set_ends(jax.random.randint(key_list[2], (NN,), 0, NBINS), jax.random.fold_in(key_list[2], 1), 0, NBINS - 1).astype(jnp.int32)
    return {"noise": noise, "data": data, "timestep": timestep}


EPS = 0.002


def row_lse(scores):
    peak = jnp.max(scores, axis=1)
    total = jnp.sum(jnp.exp(scores - peak[:, None]), axis=1)
    return peak + jnp.log(total)


def col_lse(scores):
    peak = jnp.max(scores, axis=0)
    total = jnp.sum(jnp.exp(scores - peak[None, :]), axis=0)
    return peak + jnp.log(total)


def reference(noise, data, timestep):
    noise_f = noise.astype(jnp.float32)
    data_f = data.astype(jnp.float32)
    sq_noise = jnp.sum(noise_f * noise_f, axis=1)
    sq_data = jnp.sum(data_f * data_f, axis=1)
    cross = jnp.dot(noise, data.T, preferred_element_type=jnp.float32)
    cost = (sq_noise[:, None] + sq_data[None, :] - 2.0 * cross) / DL
    g_pot = jnp.zeros((data.shape[0],), jnp.float32)
    for step in range(ITERS):
        f_pot = -EPS * row_lse((g_pot[None, :] - cost) / EPS)
        g_pot = -EPS * col_lse((f_pot[:, None] - cost) / EPS)
    scores = (g_pot[None, :] - cost) / EPS
    final = row_lse(scores)
    weights = jnp.exp(scores - final[:, None]).astype(jnp.bfloat16)
    targets = jnp.dot(weights, data, preferred_element_type=jnp.float32)
    t_val = (timestep.astype(jnp.float32) + 0.5) / NBINS
    inputs_t = ((1.0 - t_val)[:, None] * noise_f + t_val[:, None] * targets).astype(jnp.bfloat16)
    velocity = (targets - noise_f).astype(jnp.bfloat16)
    return inputs_t, velocity
```

```python
import functools

import jax
import jax.numpy as jnp
from jax import lax
from jax.experimental import pallas as pl
from jax.experimental.pallas import tpu as pltpu
from jax.sharding import PartitionSpec as P

ITERS = 4
NBINS = 1000
EPS = 0.002
LOG2E = 1.4426950408889634
MESH = pl.DeviceIdType.MESH
VMEM = pltpu.VMEM
F32 = jnp.float32
BF16 = jnp.bfloat16


def place():
    n, d = lax.axis_index("noise"), lax.axis_index("dp")
    return n, d, n // 8, (n // 2) % 4, n % 2, d // 4, d % 4


def greet(peers):
    barrier = pltpu.get_barrier_semaphore()
    for peer in peers:
        pl.semaphore_signal(barrier, inc=1, device_id=peer, device_id_type=MESH)
    return barrier


def remote(src, dst, send, recv, peer):
    return pltpu.make_async_remote_copy(
        src_ref=src, dst_ref=dst, send_sem=send, recv_sem=recv, device_id=peer, device_id_type=MESH
    )


def b2i(cond):
    return jnp.where(cond, 1, 0).astype(jnp.int32)


def cost_kernel(scale, noise_ref, data_ref, s_ref, buf, part, half, xin, zin, own, tot,
                first_send, arrive, send, c_send, c_recv, x_send, x_recv, z_send, z_recv,
                gx_send, gx_recv, gc_send, gc_recv):
    n, d, zh, x, c, zl, y = place()
    other = (n + 1 - 2 * c, d)
    far = (lax.rem(n + 8, 16), d)

    def xpeer(k):
        return zh * 8 + lax.rem(x + k, 4) * 2 + c

    up = (n, lax.rem(zl + 1, 8) * 4 + y)
    down = (n, lax.rem(zl + 7, 8) * 4 + y)
    yup = (n, zl * 4 + lax.rem(y + 1, 4))
    ydown = (n, zl * 4 + lax.rem(y + 3, 4))
    head_n, head_d, head_h = d // 2, 28 * c + y, y % 2
    mine = jnp.logical_and(head_n == n, head_d == d)
    is_head = jnp.logical_and(c == y // 2, jnp.logical_or(zl == 0, zl == 7))

    barrier = greet([other, far, up, down, yup, ydown] + [(xpeer(k), d) for k in (1, 2, 3)])

    src_d = (4 * zh + x) * 4 + y
    src_c = zl // 7

    @pl.when(is_head)
    def _():
        for k in range(8):
            src_n = k * 2 + src_c

            @pl.when(jnp.logical_not(jnp.logical_and(src_n == n, src_d == d)))
            def _():
                pl.semaphore_signal(barrier, inc=1, device_id=(src_n, src_d), device_id_type=MESH)

    pl.semaphore_wait(barrier, 9 + b2i(jnp.logical_not(mine)))

    def first():
        return remote(noise_ref, buf.at[head_h, n], first_send, arrive.at[head_h, n], (head_n, head_d))

    @pl.when(jnp.logical_not(mine))
    def _():
        first().start()

    @pl.when(mine)
    def _():
        pltpu.make_async_copy(noise_ref, buf.at[head_h, n], arrive.at[head_h, n]).start()

    def landed(h, b):
        pltpu.make_async_copy(noise_ref, buf.at[h, b], arrive.at[h, b]).wait()

    def hop(h, b, kind, peer):
        return remote(buf.at[h, b], buf.at[h, b], send.at[h, b, kind], arrive.at[h, b], peer)

    def forwards(h, b, j, direction, act):
        r = lax.rem(y - (2 * c + h) + 4, 4)
        on_chain = r == 0
        if direction == 0:
            more, nxt = zl < 7, up
        else:
            more, nxt = zl > 0, down

        @pl.when(jnp.logical_and(on_chain, more))
        def _():
            act(hop(h, b, 0, nxt))

        @pl.when(jnp.logical_or(on_chain, jnp.logical_and(r == 1, j < 4)))
        def _():
            act(hop(h, b, 1, yup))

        @pl.when(jnp.logical_or(on_chain, jnp.logical_and(r == 3, j >= 4)))
        def _():
            act(hop(h, b, 2, ydown))

    def tick(t, carry):
        for direction in (0, 1):
            pos = zl if direction == 0 else 7 - zl
            for h in (0, 1):
                r = lax.rem(y - (2 * c + h) + 4, 4)
                j = t - pos - b2i(r != 0)

                @pl.when(jnp.logical_and(r != 2, jnp.logical_and(j >= 0, j < 8)))
                def _():
                    b = 2 * j + direction
                    landed(h, b)
                    forwards(h, b, j, direction, lambda cp: cp.start())
        return carry

    lax.fori_loop(0, 16, tick, 0)

    def rest(j, carry):
        for direction in (0, 1):
            for h in (0, 1):
                r = lax.rem(y - (2 * c + h) + 4, 4)
                b = 2 * j + direction

                @pl.when(r == 2)
                def _():
                    landed(h, b)

                forwards(h, b, j, direction, lambda cp: cp.wait_send())
        return carry

    lax.fori_loop(0, 8, rest, 0)

    @pl.when(jnp.logical_not(mine))
    def _():
        first().wait_send()

    data = data_ref[...]
    dsq = jnp.sum(jnp.square(data.astype(F32)), axis=1, keepdims=True)
    ones = jnp.ones((8, 512), BF16)

    def block(b, carry):
        acc = jnp.broadcast_to(dsq, (256, 128))
        nsq = jnp.zeros((8, 128), F32)
        for h in (0, 1):
            piece = buf[h, pl.ds(2 * b, 2)].reshape(128, 512)
            acc -= 2.0 * lax.dot_general(
                data_ref[:, 512 * h:512 * (h + 1)], piece, (((1,), (1,)), ((), ())), preferred_element_type=F32
            )
            wide = piece.astype(F32)
            sq = wide * wide
            hi = sq.astype(BF16)
            lo = (sq - hi.astype(F32)).astype(BF16)
            for v in (hi, lo):
                nsq += lax.dot_general(ones, v, (((1,), (1,)), ((), ())), preferred_element_type=F32)
        part[b] = (acc + nsq[0:1, :]) * scale
        return carry

    lax.fori_loop(0, 8, block, 0)

    cp = remote(part.at[pl.ds(4 * (1 - c), 4)], half, c_send, c_recv, other)
    cp.start()
    cp.wait()
    for k in range(4):
        half[k] = half[k] + part[4 * c + k]
    for k in (1, 2, 3):
        t = lax.rem(x + k, 4)
        remote(half.at[t], xin.at[x], x_send.at[k], x_recv.at[x], (xpeer(k), d)).start()
    acc = half[x]
    for k in (1, 2, 3):
        t = lax.rem(x + k, 4)
        remote(half.at[t], xin.at[t], x_send.at[k], x_recv.at[t], (xpeer(k), d)).wait()
        acc += xin[t]
    own[...] = acc
    cp = remote(own, zin, z_send, z_recv, far)
    cp.start()
    cp.wait()
    tot[4 * c + x] = own[...] + zin[...]
    mineb = tot.at[4 * c + x]
    for k in (1, 2, 3):
        remote(mineb, mineb, gx_send.at[k], gx_recv.at[x], (xpeer(k), d)).start()
    for k in (1, 2, 3):
        t = lax.rem(x + k, 4)
        remote(mineb, tot.at[4 * c + t], gx_send.at[k], gx_recv.at[t], (xpeer(k), d)).wait()
    cp = remote(tot.at[pl.ds(4 * c, 4)], tot.at[pl.ds(4 * c, 4)], gc_send, gc_recv, other)
    cp.start()
    cp.wait_send()
    remote(tot.at[pl.ds(4 * (1 - c), 4)], tot.at[pl.ds(4 * (1 - c), 4)], gc_send, gc_recv, other).wait_recv()
    s_ref[...] = tot[...]


def sinkhorn_kernel(s_ref, data_ref, w_ref, dt_ref, gpot, row, rz, ry, zs, zr, ys, yr, as_, ar, loc):
    n, d, zh, x, c, zl, y = place()

    def zp(k):
        return lax.rem(zl + k, 8)

    def yp(k):
        return lax.rem(y + k, 4)

    zpeers = [(n, zp(k) * 4 + y) for k in range(1, 8)]
    ypeers = [(n, zl * 4 + yp(k)) for k in range(1, 4)]
    dests = []
    for h in (0, 1):
        for cc in (0, 1):
            dests.append((h, cc, (zh * 8 + x * 2 + cc, zl * 4 + 2 * c + h)))
    srcc = y // 2
    srcs = [(zh * 8 + x * 2 + srcc, zl * 4 + k) for k in range(4)]
    barrier = greet(zpeers + ypeers)
    for k in range(4):
        same = jnp.logical_and(srcc == c, y == k)

        @pl.when(jnp.logical_not(same))
        def _():
            pl.semaphore_signal(barrier, inc=1, device_id=srcs[k], device_id_type=MESH)

    count = 10
    for h, cc, _ in dests:
        count = count + 1 - b2i(jnp.logical_and(c == cc, y == 2 * c + h))
    pl.semaphore_wait(barrier, count)

    def spread(h, cc, peer, act):
        same = jnp.logical_and(c == cc, y == 2 * c + h)
        src = data_ref.at[:, pl.ds(512 * h, 512)]

        @pl.when(jnp.logical_not(same))
        def _():
            act(remote(src, dt_ref.at[y], as_.at[h, cc], ar.at[y], peer))

        @pl.when(same)
        def _():
            act(pltpu.make_async_copy(src, dt_ref.at[y], loc), True)

    for h, cc, peer in dests:
        spread(h, cc, peer, lambda cp, own=False: cp.start())

    gpot[...] = jnp.zeros_like(gpot)

    def rows(k):
        g = gpot[...]
        for b in range(8):
            v = g - s_ref[b]
            m = jnp.max(v, axis=0, keepdims=True)
            row[k, b:b + 1, :] = m + jnp.log2(jnp.sum(jnp.exp2(v - m), axis=0, keepdims=True))
        for i, peer in enumerate(zpeers):
            remote(row.at[k], rz.at[k, zl], zs.at[k, i], zr.at[k, zl], peer).start()
        rz[k, zl] = row[k]
        for i, peer in enumerate(zpeers):
            remote(row.at[k], rz.at[k, zp(i + 1)], zs.at[k, i], zr.at[k, zp(i + 1)], peer).wait()
        v = rz[k]
        m = jnp.max(v, axis=0)
        ry[k, y] = m + jnp.log2(jnp.sum(jnp.exp2(v - m[None]), axis=0))
        mine = ry.at[k, y]
        for i, peer in enumerate(ypeers):
            remote(mine, mine, ys.at[k, i], yr.at[k, y], peer).start()
        for i, peer in enumerate(ypeers):
            remote(mine, ry.at[k, yp(i + 1)], ys.at[k, i], yr.at[k, yp(i + 1)], peer).wait()
        v = ry[k]
        m = jnp.max(v, axis=0)
        return m + jnp.log2(jnp.sum(jnp.exp2(v - m[None]), axis=0))

    def iteration(k, carry):
        lse = rows(k)
        m = (-lse[0:1]) - s_ref[0]
        for b in range(1, 8):
            m = jnp.maximum(m, (-lse[b:b + 1]) - s_ref[b])
        m = jnp.broadcast_to(jnp.max(m, axis=1, keepdims=True), (256, 128))
        tot = jnp.zeros((256, 128), F32)
        for b in range(8):
            tot += jnp.exp2((-lse[b:b + 1]) - s_ref[b] - m)
        tot = jnp.broadcast_to(jnp.sum(tot, axis=1, keepdims=True), (256, 128))
        gpot[...] = -(m + jnp.log2(tot))
        return carry

    lax.fori_loop(0, ITERS, iteration, 0)
    lse = rows(ITERS)
    g = gpot[...]
    for b in range(8):
        w_ref[b] = jnp.exp2(g - s_ref[b] - lse[b:b + 1]).astype(BF16)

    for h, cc, peer in dests:
        spread(h, cc, peer, lambda cp, own=False: cp.wait() if own else cp.wait_send())
    for k in range(4):
        same = jnp.logical_and(srcc == c, y == k)

        @pl.when(jnp.logical_not(same))
        def _():
            remote(dt_ref.at[k], dt_ref.at[k], as_.at[0, 0], ar.at[k], srcs[k]).wait_recv()


def target_kernel(w_ref, dt_ref, t_ref, wbuf, part, inbox, stage, got, ws, wr, cs, cr, fs, fr):
    n, d, zh, x, c, zl, y = place()
    up = (n, lax.rem(zl + 1, 8) * 4 + y)
    down = (n, lax.rem(zl + 7, 8) * 4 + y)
    yup = (n, zl * 4 + lax.rem(y + 1, 4))
    ydown = (n, zl * 4 + lax.rem(y + 3, 4))
    out_d = 16 * zh + 4 * x + y
    from_n = (zl // 4) * 8 + (zl % 4) * 2 + zh
    from_d = 28 * (1 - c) + y
    from_self = jnp.logical_and(from_n == n, from_d == d)
    barrier = greet([up, down, yup, ydown])

    @pl.when(jnp.logical_not(from_self))
    def _():
        pl.semaphore_signal(barrier, inc=1, device_id=(from_n, from_d), device_id_type=MESH)

    is_end = jnp.logical_or(zl == 0, zl == 7)
    self_end = b2i(jnp.logical_and(is_end, from_self))
    pl.semaphore_wait(barrier, 4 + 4 * b2i(is_end) - self_end)

    rows4 = pl.ds(4 * c, 4)
    mine = w_ref.at[rows4]

    def wsend(q, dst_y, k, peer):
        src = mine if dst_y is None else wbuf.at[dst_y]
        slot = wbuf.at[y] if dst_y is None else wbuf.at[dst_y]
        lo = pl.ds(2 * q, 2)
        return remote(src.at[lo], slot.at[lo], ws.at[k, q], wr.at[y if dst_y is None else dst_y, q], peer)

    left, right, across = lax.rem(y + 3, 4), lax.rem(y + 1, 4), lax.rem(y + 2, 4)
    for q in (0, 1):
        wsend(q, None, 0, yup).start()
    for q in (1, 0):
        wsend(q, None, 1, ydown).start()
    wbuf[y] = w_ref[rows4]

    def wwait(src_y, q):
        lo = pl.ds(2 * q, 2)
        remote(mine.at[lo], wbuf.at[src_y].at[lo], ws.at[0, q], wr.at[src_y, q], yup).wait_recv()

    wwait(left, 0)
    wsend(0, left, 2, yup).start()
    wwait(right, 1)
    wsend(1, right, 3, ydown).start()
    wwait(left, 1)
    wwait(right, 0)
    wwait(across, 0)
    wwait(across, 1)

    def mul(b, carry):
        acc = jnp.zeros((128, 512), F32)
        for k in range(4):
            acc += lax.dot_general(
                wbuf[k, b], dt_ref[k], (((0,), (0,)), ((), ())), preferred_element_type=F32
            )
        part[pl.ds(2 * b, 2)] = acc.reshape(2, 64, 512)
        return carry

    lax.fori_loop(0, 4, mul, 0)

    def hop(b, direction):
        return remote(stage.at[b], inbox.at[b], cs.at[b], cr.at[b], up if direction == 0 else down)

    def final(b):
        return remote(stage.at[b], got, fs.at[b], fr, (8 * c + b, out_d))

    def own_end(b):
        return jnp.logical_and(n == 8 * c + b, d == out_d)

    def tick(t, carry):
        for direction in (0, 1):
            pos = zl if direction == 0 else 7 - zl
            j = t - pos
            b = 2 * j + direction

            @pl.when(jnp.logical_and(j >= 0, j < 4))
            def _():
                @pl.when(pos == 0)
                def _():
                    stage[b] = part[b].astype(BF16)

                @pl.when(pos > 0)
                def _():
                    hop(b, direction).wait_recv()
                    stage[b] = (part[b] + inbox[b].astype(F32)).astype(BF16)

                @pl.when(pos < 7)
                def _():
                    hop(b, direction).start()

                @pl.when(pos == 7)
                def _():
                    @pl.when(jnp.logical_not(own_end(b)))
                    def _():
                        final(b).start()

                    @pl.when(own_end(b))
                    def _():
                        pltpu.make_async_copy(stage.at[b], got, fr).start()
        return carry

    lax.fori_loop(0, 11, tick, 0)
    pltpu.make_async_copy(stage.at[0], got, fr).wait()
    t_ref[...] = got[...]

    def drain(j, carry):
        for direction in (0, 1):
            pos = zl if direction == 0 else 7 - zl
            b = 2 * j + direction

            @pl.when(pos < 7)
            def _():
                hop(b, direction).wait_send()

            @pl.when(jnp.logical_and(pos == 7, jnp.logical_not(own_end(b))))
            def _():
                final(b).wait_send()
        return carry

    lax.fori_loop(0, 4, drain, 0)
    for q in (0, 1):
        wsend(q, None, 0, yup).wait_send()
        wsend(q, None, 1, ydown).wait_send()
    wsend(0, left, 2, yup).wait_send()
    wsend(1, right, 3, ydown).wait_send()


def whole():
    return pl.BlockSpec(memory_space=pltpu.VMEM)


def params(cid):
    return pltpu.CompilerParams(collective_id=cid, has_side_effects=True, vmem_limit_bytes=40 * 1024 * 1024)


DMA = pltpu.SemaphoreType.DMA


def cost_call(noise, data):
    scale = LOG2E / (16384.0 * EPS)
    return pl.pallas_call(
        functools.partial(cost_kernel, scale),
        out_shape=jax.ShapeDtypeStruct((8, 256, 128), F32),
        in_specs=[whole()] * 2,
        out_specs=whole(),
        scratch_shapes=[
            VMEM((2, 16, 64, 512), BF16),
            VMEM((8, 256, 128), F32),
            VMEM((4, 256, 128), F32),
            VMEM((4, 256, 128), F32),
            VMEM((256, 128), F32),
            VMEM((256, 128), F32),
            VMEM((8, 256, 128), F32),
            DMA, DMA((2, 16)), DMA((2, 16, 3)),
            DMA, DMA, DMA((4,)), DMA((4,)), DMA, DMA,
            DMA((4,)), DMA((4,)), DMA, DMA,
        ],
        compiler_params=params(1),
    )(noise, data)


def sinkhorn_call(s, data):
    return pl.pallas_call(
        sinkhorn_kernel,
        out_shape=[jax.ShapeDtypeStruct((8, 256, 128), BF16), jax.ShapeDtypeStruct((4, 256, 512), BF16)],
        in_specs=[whole()] * 2,
        out_specs=[whole()] * 2,
        scratch_shapes=[
            VMEM((256, 128), F32),
            VMEM((ITERS + 1, 8, 128), F32),
            VMEM((ITERS + 1, 8, 8, 128), F32),
            VMEM((ITERS + 1, 4, 8, 128), F32),
            DMA((ITERS + 1, 7)), DMA((ITERS + 1, 8)),
            DMA((ITERS + 1, 3)), DMA((ITERS + 1, 4)),
            DMA((2, 2)), DMA((4,)), DMA,
        ],
        compiler_params=params(2),
    )(s, data)


def target_call(w, dt):
    return pl.pallas_call(
        target_kernel,
        out_shape=jax.ShapeDtypeStruct((64, 512), BF16),
        in_specs=[whole()] * 2,
        out_specs=whole(),
        scratch_shapes=[
            VMEM((4, 4, 256, 128), BF16),
            VMEM((8, 64, 512), F32),
            VMEM((8, 64, 512), BF16),
            VMEM((8, 64, 512), BF16),
            VMEM((64, 512), BF16),
            DMA((4, 2)), DMA((4, 2)),
            DMA((8,)), DMA((8,)), DMA((8,)), DMA,
        ],
        compiler_params=params(3),
    )(w, dt)


def per_device(noise, data, timestep):
    s = cost_call(noise, data)
    w, dt = sinkhorn_call(s, data)
    targets = target_call(w, dt).astype(F32)
    noise_f = noise.astype(F32)
    t_val = (timestep.astype(F32) + 0.5) / NBINS
    inputs_t = ((1.0 - t_val)[:, None] * noise_f + t_val[:, None] * targets).astype(BF16)
    velocity = (targets - noise_f).astype(BF16)
    return (inputs_t, velocity)


def solution(mesh):
    placed = (P("noise", "dp"), P("dp", "noise"), P("noise"))
    return jax.shard_map(
        per_device,
        mesh=mesh,
        in_specs=placed,
        out_specs=(P("noise", "dp"), P("noise", "dp")),
        check_vma=False,
    )
```

```python
import functools

import jax
import jax.numpy as jnp
from jax import lax
from jax.experimental import pallas as pl
from jax.experimental.pallas import tpu as pltpu
from jax.sharding import PartitionSpec as P

ITERS = 4
NBINS = 1000
EPS = 0.002
LOG2E = 1.4426950408889634
MESH = pl.DeviceIdType.MESH
VMEM = pltpu.VMEM
F32 = jnp.float32
BF16 = jnp.bfloat16
LAG = 4


def remote(src, dst, send, recv, peer):
    return pltpu.make_async_remote_copy(
        src_ref=src, dst_ref=dst, send_sem=send, recv_sem=recv, device_id=peer, device_id_type=MESH
    )


def b2i(cond):
    return jnp.where(cond, 1, 0).astype(jnp.int32)


def fused_kernel(scale, noise_hbm, data_hbm, out_ref,
                 noise_ref, data_ref, dsq_ref, buf, part, half, xin, own, zin, s_ref,
                 gpot, row, rz, ry, mloc, w_ref, dt_ref, wbuf, mbuf, tpart, stage, qin, fin, got,
                 load_sem, first_send, arrive, send,
                 c_send, c_recv, x_send, x_recv, z_send, z_recv, gx_send, gx_recv, gc_send, gc_recv,
                 zs, zr, ys, yr, as_, ar, loc, ws, wr, ms, mr, qs, qr, fs, fr):
    n, d = lax.axis_index("noise"), lax.axis_index("dp")
    zh, x, c, zl, y = n // 8, (n // 2) % 4, n % 2, d // 4, d % 4
    load_noise = pltpu.make_async_copy(noise_hbm, noise_ref, load_sem.at[0])
    load_data = pltpu.make_async_copy(data_hbm, data_ref, load_sem.at[1])
    load_noise.start()
    load_data.start()

    other_n = n + 1 - 2 * c
    other = (other_n, d)
    far = (lax.rem(n + 8, 16), d)

    def xq(k):
        return lax.rem(x + k, 4)

    def yq(k):
        return lax.rem(y + k, 4)

    def zq(k):
        return lax.rem(zl + k, 8)

    xpeers = [(zh * 8 + xq(k) * 2 + c, d) for k in (1, 2, 3)]
    ypeers = [(n, zl * 4 + yq(k)) for k in (1, 2, 3)]
    zpeers = [(n, zq(k) * 4 + y) for k in range(1, 8)]
    yup, ydown = ypeers[0], ypeers[2]
    across = [(other_n, zl * 4 + yq(k)) for k in (1, 2, 3)]
    zup, zdown = zpeers[0], zpeers[6]
    zi, zg = zl % 4, zl // 4

    head_n, head_h = d // 2, y % 2
    heads = [(head_n, (4 * g + 3 * c) * 4 + y) for g in (0, 1)]
    q_me = c * 8 + zh * 4 + x

    def is_me(peer):
        return jnp.logical_and(peer[0] == n, peer[1] == d)

    barrier = pltpu.get_barrier_semaphore()

    def greet(peer):
        pl.semaphore_signal(barrier, inc=1, device_id=peer, device_id_type=MESH)

    sym = [other, far] + xpeers + ypeers + zpeers + across
    for peer in sym:
        greet(peer)
    is_head = jnp.logical_and(c == y // 2, jnp.logical_or(zi == 0, zi == 3))

    @pl.when(is_head)
    def _():
        for k in range(8):
            peer = (k * 2 + zi // 3, (4 * zh + x) * 4 + y)

            @pl.when(jnp.logical_not(is_me(peer)))
            def _():
                greet(peer)

    final_from = [((zl // 4) * 8 + zi * 2 + c, (x + 4 * g) * 4 + y) for g in (0, 1)]
    final_to = [(h * 8 + zi * 2 + c, (4 * zh + x) * 4 + y) for h in (0, 1)]
    count = len(sym)
    for peer in final_from:
        @pl.when(jnp.logical_not(is_me(peer)))
        def _():
            greet(peer)
    for peer in heads + final_to:
        count = count + 1 - b2i(is_me(peer))
    load_noise.wait()
    pl.semaphore_wait(barrier, count)

    def first(g):
        return remote(noise_ref, buf.at[head_h, q_me], first_send.at[g], arrive.at[head_h, q_me], heads[g])

    for g in (0, 1):
        @pl.when(jnp.logical_not(is_me(heads[g])))
        def _():
            first(g).start()

        @pl.when(is_me(heads[g]))
        def _():
            pltpu.make_async_copy(noise_ref, buf.at[head_h, q_me], arrive.at[head_h, q_me]).start()

    load_data.wait()
    dsq_ref[...] = jnp.broadcast_to(
        jnp.sum(jnp.square(data_ref[...].astype(F32)), axis=1, keepdims=True), (256, 128)
    )

    def landed(h, q):
        pltpu.make_async_copy(noise_ref, buf.at[h, q], arrive.at[h, q]).wait()

    def hop(h, q, kind, peer):
        return remote(buf.at[h, q], buf.at[h, q], send.at[h, q, kind], arrive.at[h, q], peer)

    def around(h):
        return lax.rem(y - (2 * c + h) + 4, 4)

    def forwards(h, q, act):
        r = around(h)
        j, upward = q % 8, q < 8
        on_chain = r == 0

        @pl.when(jnp.logical_and(on_chain, jnp.logical_and(upward, zi < 3)))
        def _():
            act(hop(h, q, 0, zup))

        @pl.when(jnp.logical_and(on_chain, jnp.logical_and(jnp.logical_not(upward), zi > 0)))
        def _():
            act(hop(h, q, 0, zdown))

        @pl.when(jnp.logical_or(on_chain, jnp.logical_and(r == 1, j % 2 == 0)))
        def _():
            act(hop(h, q, 1, yup))

        @pl.when(jnp.logical_or(on_chain, jnp.logical_and(r == 3, j % 2 == 1)))
        def _():
            act(hop(h, q, 2, ydown))

    near = zi // 2

    def side(k):
        return near if k == 0 else 1 - near

    def tick(t, carry):
        for lagging in (0, 1):
            for h in (0, 1):
                r = around(h)
                s = t - LAG * lagging
                mine = r == 0 if lagging == 0 else jnp.logical_or(r == 1, r == 3)

                @pl.when(jnp.logical_and(mine, jnp.logical_and(s >= 0, s < 16)))
                def _():
                    q = 8 * jnp.where(s < 8, near, 1 - near) + s % 8
                    landed(h, q)
                    forwards(h, q, lambda cp: cp.start())
        return carry

    def last_column(k):
        def body(j, carry):
            for h in (0, 1):
                @pl.when(around(h) == 2)
                def _():
                    landed(h, 8 * side(k) + j)
            return carry

        lax.fori_loop(0, 8, body, 0)

    ones = jnp.ones((8, 512), BF16)

    def costs(k):
        def block(b, carry):
            acc = dsq_ref[...]
            nsq = jnp.zeros((8, 128), F32)
            for h in (0, 1):
                piece = buf[h, pl.ds(8 * side(k) + 2 * b, 2)].reshape(128, 512)
                acc -= 2.0 * lax.dot_general(
                    data_ref[:, 512 * h:512 * (h + 1)], piece, (((1,), (1,)), ((), ())), preferred_element_type=F32
                )
                wide = piece.astype(F32)
                sq = wide * wide
                hi = sq.astype(BF16)
                lo = (sq - hi.astype(F32)).astype(BF16)
                for v in (hi, lo):
                    nsq += lax.dot_general(ones, v, (((1,), (1,)), ((), ())), preferred_element_type=F32)
            part[side(k), b] = (acc + nsq[0:1, :]) * scale
            return carry

        lax.fori_loop(0, 4, block, 0)

    def core_sum(k):
        return remote(part.at[side(k), :, pl.ds(128 * (1 - c), 128)], half.at[k], c_send.at[k], c_recv.at[k], other)

    def core_done(k):
        core_sum(k).wait()
        half[k] = half[k] + part[side(k), :, pl.ds(pl.multiple_of(128 * c, 128), 128)]

    def x_sum(k, i, slot):
        return remote(
            half.at[k, :, pl.ds(32 * xq(i), 32)], xin.at[k, slot], x_send.at[k, i], x_recv.at[k, slot], xpeers[i - 1]
        )

    def x_start(k):
        for i in (1, 2, 3):
            x_sum(k, i, x).start()

    def x_done(k):
        acc = half[k, :, pl.ds(pl.multiple_of(32 * x, 32), 32)]
        for i in (1, 2, 3):
            x_sum(k, i, xq(i)).wait()
            acc += xin[k, xq(i)]
        own[k] = acc

    def z_sum(k):
        return remote(own.at[k], zin.at[k], z_send.at[k], z_recv.at[k], far)

    def slab(k, cc, xx):
        return s_ref.at[pl.ds(4 * side(k), 4), pl.ds(128 * cc + 32 * xx, 32)]

    def z_done(k):
        z_sum(k).wait()
        s_ref[pl.ds(4 * side(k), 4), pl.ds(pl.multiple_of(128 * c + 32 * x, 32), 32)] = own[k] + zin[k]
        for i in (1, 2, 3):
            remote(slab(k, c, x), slab(k, c, x), gx_send.at[k, i], gx_recv.at[k, x], xpeers[i - 1]).start()

    def core_slab(k, cc):
        return s_ref.at[pl.ds(4 * side(k), 4), pl.ds(128 * cc, 128)]

    def core_gather(k, cc):
        return remote(core_slab(k, cc), core_slab(k, cc), gc_send.at[k], gc_recv.at[k], other)

    def gx_done(k):
        for i in (1, 2, 3):
            remote(slab(k, c, x), slab(k, c, xq(i)), gx_send.at[k, i], gx_recv.at[k, xq(i)], xpeers[i - 1]).wait()
        core_gather(k, c).start()

    def gc_done(k):
        core_gather(k, c).wait_send()
        core_gather(k, 1 - c).wait_recv()

    srcc = y // 2

    def spread(act):
        for h in (0, 1):
            for cc in (0, 1):
                same = jnp.logical_and(c == cc, y == 2 * c + h)
                src = data_ref.at[:, pl.ds(512 * h, 512)]

                @pl.when(jnp.logical_not(same))
                def _():
                    peer = (zh * 8 + x * 2 + cc, zl * 4 + 2 * c + h)
                    act(remote(src, dt_ref.at[y], as_.at[h, cc], ar.at[y], peer), False)

                @pl.when(same)
                def _():
                    act(pltpu.make_async_copy(src, dt_ref.at[y], loc), True)

    lax.fori_loop(0, 8 + LAG, tick, 0)
    last_column(0)
    costs(0)
    core_sum(0).start()
    lax.fori_loop(8 + LAG, 12 + LAG, tick, 0)
    core_done(0)
    x_start(0)
    lax.fori_loop(12 + LAG, 16 + LAG, tick, 0)
    last_column(1)
    costs(1)
    core_sum(1).start()
    x_done(0)
    z_sum(0).start()
    core_done(1)
    x_start(1)
    spread(lambda cp, local: cp.start())
    x_done(1)
    z_sum(1).start()
    z_done(0)
    gx_done(0)
    z_done(1)
    gx_done(1)
    gc_done(0)
    gc_done(1)

    gpot[...] = jnp.zeros_like(gpot)

    def lse0(v):
        m = jnp.max(v, axis=0)
        return m + jnp.log2(jnp.sum(jnp.exp2(v - m[None]), axis=0))

    def z_rows(k):
        for i, peer in enumerate(zpeers):
            remote(row.at[k], rz.at[k, zl], zs.at[k, i], zr.at[k, zl], peer).start()
        rz[k, zl] = row[k]

    def all_rows(k):
        for i, peer in enumerate(zpeers):
            remote(row.at[k], rz.at[k, zq(i + 1)], zs.at[k, i], zr.at[k, zq(i + 1)], peer).wait()
        ry[k, y] = lse0(rz[k])
        mine = ry.at[k, y]
        for i, peer in enumerate(ypeers):
            remote(mine, mine, ys.at[k, i], yr.at[k, y], peer).start()
        for i, peer in enumerate(ypeers):
            remote(mine, ry.at[k, yq(i + 1)], ys.at[k, i], yr.at[k, yq(i + 1)], peer).wait()
        return lse0(ry[k])

    def iteration(k, carry):
        g = gpot[...]
        for b in range(8):
            v = g - s_ref[b]
            m = jnp.max(v, axis=0, keepdims=True)
            row[k, b:b + 1, :] = m + jnp.log2(jnp.sum(jnp.exp2(v - m), axis=0, keepdims=True))
        z_rows(k)
        f = -all_rows(k)
        m = f[0:1] - s_ref[0]
        for b in range(1, 8):
            m = jnp.maximum(m, f[b:b + 1] - s_ref[b])
        m = jnp.broadcast_to(jnp.max(m, axis=1, keepdims=True), (256, 128))
        tot = jnp.zeros((256, 128), F32)
        for b in range(8):
            tot += jnp.exp2(f[b:b + 1] - s_ref[b] - m)
        tot = jnp.broadcast_to(jnp.sum(tot, axis=1, keepdims=True), (256, 128))
        gpot[...] = -(m + jnp.log2(tot))
        return carry

    lax.fori_loop(0, ITERS, iteration, 0)

    g = gpot[...]
    for b in range(8):
        v = g - s_ref[b]
        m = jnp.max(v, axis=0, keepdims=True)
        e = jnp.exp2(v - m)
        w_ref[b] = e.astype(BF16)
        mloc[b:b + 1, :] = m
        row[ITERS, b:b + 1, :] = m + jnp.log2(jnp.sum(e, axis=0, keepdims=True))

    def wsend(b, k, peer):
        return remote(w_ref.at[4 * c + b], wbuf.at[y, b], ws.at[k, b], wr.at[y, b], peer)

    def wpass(b, src, k, peer):
        return remote(wbuf.at[src, b], wbuf.at[src, b], ws.at[k, b], wr.at[src, b], peer)

    def wwait(b, src):
        remote(w_ref.at[b], wbuf.at[src, b], ws.at[0, b], wr.at[src, b], yup).wait_recv()

    left, right, opposite = yq(3), yq(1), yq(2)
    z_rows(ITERS)
    for i, peer in enumerate(ypeers):
        remote(mloc, mbuf.at[y], ms.at[i], mr.at[y], peer).start()
    for b in range(4):
        wsend(b, 0, yup).start()
        wsend(b, 1, ydown).start()
    wbuf[y] = w_ref[pl.ds(4 * c, 4)]
    mbuf[y] = mloc[...]
    for b in range(4):
        if b % 2 == 0:
            wwait(b, left)
            wpass(b, left, 2, yup).start()
        else:
            wwait(b, right)
            wpass(b, right, 2, ydown).start()
    for i, peer in enumerate(ypeers):
        remote(mloc, mbuf.at[yq(i + 1)], ms.at[i], mr.at[yq(i + 1)], peer).wait()
    lse = all_rows(ITERS)
    spread(lambda cp, local: cp.wait() if local else cp.wait_send())
    for k in range(4):
        @pl.when(jnp.logical_not(jnp.logical_and(srcc == c, y == k)))
        def _():
            peer = (zh * 8 + x * 2 + srcc, zl * 4 + k)
            remote(dt_ref.at[k], dt_ref.at[k], as_.at[0, 0], ar.at[k], peer).wait_recv()
    factor = [jnp.transpose(jnp.exp2(mbuf[k] - lse)) for k in range(4)]

    def quad(i):
        return (n, (4 * zg + (zi + i) % 4) * 4 + y)

    def quad_sum(h, i, slot):
        return remote(stage.at[h, (zi + i) % 4], qin.at[h, slot], qs.at[h, i], qr.at[h, slot], quad(i))

    for h in (0, 1):
        for bb in (0, 1):
            b = 2 * h + bb
            if b % 2 == 0:
                wwait(b, right)
            else:
                wwait(b, left)
            wwait(b, opposite)
            acc = jnp.zeros((128, 512), F32)
            for k in range(4):
                fk = jnp.where(c == 0, factor[k][:, b:b + 1], factor[k][:, 4 + b:5 + b])
                acc += fk * lax.dot_general(
                    wbuf[k, b], dt_ref[k], (((0,), (0,)), ((), ())), preferred_element_type=F32
                )
            tpart[h, 2 * bb:2 * bb + 2] = acc.reshape(2, 64, 512)
            stage[h, 2 * bb:2 * bb + 2] = acc.reshape(2, 64, 512).astype(BF16)
        for i in (1, 2, 3):
            quad_sum(h, i, zi).start()

    def final(h):
        return remote(fin.at[h], got.at[zg], fs.at[h], fr.at[zg], final_to[h])

    for h in (0, 1):
        acc = tpart[h, zi]
        for i in (1, 2, 3):
            quad_sum(h, i, (zi + i) % 4).wait()
            acc += qin[h, (zi + i) % 4].astype(F32)
        fin[h] = acc.astype(BF16)

        @pl.when(jnp.logical_not(is_me(final_to[h])))
        def _():
            final(h).start()

        @pl.when(is_me(final_to[h]))
        def _():
            pltpu.make_async_copy(fin.at[h], got.at[zg], fr.at[zg]).start()

    for g in (0, 1):
        @pl.when(jnp.logical_not(is_me(heads[g])))
        def _():
            first(g).wait_send()

    def drain(q, carry):
        for h in (0, 1):
            forwards(h, q, lambda cp: cp.wait_send())
        return carry

    lax.fori_loop(0, 16, drain, 0)
    for b in range(4):
        wsend(b, 0, yup).wait_send()
        wsend(b, 1, ydown).wait_send()
        if b % 2 == 0:
            wpass(b, left, 2, yup).wait_send()
        else:
            wpass(b, right, 2, ydown).wait_send()
    for g in (0, 1):
        pltpu.make_async_copy(fin.at[0], got.at[g], fr.at[g]).wait()
    out_ref[...] = got[0].astype(F32) + got[1].astype(F32)
    for h in (0, 1):
        @pl.when(jnp.logical_not(is_me(final_to[h])))
        def _():
            final(h).wait_send()


DMA = pltpu.SemaphoreType.DMA


def fused_call(noise, data):
    scale = LOG2E / (16384.0 * EPS)
    rounds = ITERS + 1
    return pl.pallas_call(
        functools.partial(fused_kernel, scale),
        out_shape=jax.ShapeDtypeStruct((64, 512), F32),
        in_specs=[pl.BlockSpec(memory_space=pl.ANY)] * 2,
        out_specs=pl.BlockSpec(memory_space=VMEM),
        scratch_shapes=[
            VMEM((64, 512), BF16), VMEM((256, 1024), BF16), VMEM((256, 128), F32),
            VMEM((2, 16, 64, 512), BF16),
            VMEM((2, 4, 256, 128), F32), VMEM((2, 4, 128, 128), F32), VMEM((2, 4, 4, 32, 128), F32),
            VMEM((2, 4, 32, 128), F32), VMEM((2, 4, 32, 128), F32), VMEM((8, 256, 128), F32),
            VMEM((256, 128), F32), VMEM((rounds, 8, 128), F32), VMEM((rounds, 8, 8, 128), F32),
            VMEM((rounds, 4, 8, 128), F32), VMEM((8, 128), F32),
            VMEM((8, 256, 128), BF16), VMEM((4, 256, 512), BF16), VMEM((4, 4, 256, 128), BF16),
            VMEM((4, 8, 128), F32),
            VMEM((2, 4, 64, 512), F32), VMEM((2, 4, 64, 512), BF16), VMEM((2, 4, 64, 512), BF16),
            VMEM((2, 64, 512), BF16), VMEM((2, 64, 512), BF16),
            DMA((2,)), DMA((2,)), DMA((2, 16)), DMA((2, 16, 3)),
            DMA((2,)), DMA((2,)), DMA((2, 4)), DMA((2, 4)), DMA((2,)), DMA((2,)),
            DMA((2, 4)), DMA((2, 4)), DMA((2,)), DMA((2,)),
            DMA((rounds, 7)), DMA((rounds, 8)), DMA((rounds, 3)), DMA((rounds, 4)),
            DMA((2, 2)), DMA((4,)), DMA, DMA((3, 4)), DMA((4, 4)), DMA((3,)), DMA((4,)),
            DMA((2, 4)), DMA((2, 4)), DMA((2,)), DMA((2,)),
        ],
        compiler_params=pltpu.CompilerParams(
            collective_id=1, has_side_effects=True, vmem_limit_bytes=40 * 1024 * 1024
        ),
    )(noise, data)


def per_device(noise, data, timestep):
    targets = fused_call(noise, data)
    noise_f = noise.astype(F32)
    t_val = (timestep.astype(F32) + 0.5) / NBINS
    inputs_t = ((1.0 - t_val)[:, None] * noise_f + t_val[:, None] * targets).astype(BF16)
    velocity = (targets - noise_f).astype(BF16)
    return (inputs_t, velocity)


def solution(mesh):
    placed = (P("noise", "dp"), P("dp", "noise"), P("noise"))
    return jax.shard_map(
        per_device,
        mesh=mesh,
        in_specs=placed,
        out_specs=(P("noise", "dp"), P("noise", "dp")),
        check_vma=False,
    )
```

```python
import functools

import jax
import jax.numpy as jnp
from jax import lax
from jax.experimental import pallas as pl
from jax.experimental.pallas import tpu as pltpu
from jax.sharding import PartitionSpec as P

ITERS = 4
NBINS = 1000
EPS = 0.002
LOG2E = 1.4426950408889634
MESH = pl.DeviceIdType.MESH
VMEM = pltpu.VMEM
F32 = jnp.float32
BF16 = jnp.bfloat16
LAG = 4
DIRECT = (False, False)


def remote(src, dst, send, recv, peer):
    return pltpu.make_async_remote_copy(
        src_ref=src, dst_ref=dst, send_sem=send, recv_sem=recv, device_id=peer, device_id_type=MESH
    )


def b2i(cond):
    return jnp.where(cond, 1, 0).astype(jnp.int32)


def fused_kernel(scale, noise_hbm, data_hbm, step_ref, out_ref, time_ref,
                 noise_ref, data_ref, dsq_ref, buf, part, half, xin, own, zin, s_ref,
                 gpot, fpot, row, rz, ry, w_ref, dt_ref, wbuf, tpart, stage, qin, fin, got,
                 load_sem, first_send, arrive, send,
                 c_send, c_recv, x_send, x_recv, z_send, z_recv, gx_send, gx_recv, gc_send, gc_recv,
                 zs, zr, ys, yr, as_, ar, loc, ws, wr, qs, qr, fs, fr):
    n, d = lax.axis_index("noise"), lax.axis_index("dp")
    zh, x, c, zl, y = n // 8, (n // 2) % 4, n % 2, d // 4, d % 4
    load_noise = pltpu.make_async_copy(noise_hbm, noise_ref, load_sem.at[0])
    load_data = pltpu.make_async_copy(data_hbm, data_ref, load_sem.at[1])
    load_noise.start()
    load_data.start()

    other_n = n + 1 - 2 * c
    other = (other_n, d)
    far = (lax.rem(n + 8, 16), d)

    def xq(k):
        return lax.rem(x + k, 4)

    def yq(k):
        return lax.rem(y + k, 4)

    def zq(k):
        return lax.rem(zl + k, 8)

    xpeers = [(zh * 8 + xq(k) * 2 + c, d) for k in (1, 2, 3)]
    ypeers = [(n, zl * 4 + yq(k)) for k in (1, 2, 3)]
    zpeers = [(n, zq(k) * 4 + y) for k in range(1, 8)]
    yup, ydown = ypeers[0], ypeers[2]
    across = [(other_n, zl * 4 + yq(k)) for k in (1, 2, 3)]
    zup, zdown = zpeers[0], zpeers[6]
    zi, zg = zl % 4, zl // 4

    head_n, head_h = d // 2, y % 2
    heads = [(head_n, (4 * g + 1 + c) * 4 + y) for g in (0, 1)]
    q_me = c * 8 + zh * 4 + x

    def is_me(peer):
        return jnp.logical_and(peer[0] == n, peer[1] == d)

    barrier = pltpu.get_barrier_semaphore()

    def greet(peer):
        pl.semaphore_signal(barrier, inc=1, device_id=peer, device_id_type=MESH)

    sym = [other, far] + xpeers + ypeers + zpeers + across
    for peer in sym:
        greet(peer)
    is_head = jnp.logical_and(c == y // 2, jnp.logical_or(zi == 1, zi == 2))

    @pl.when(is_head)
    def _():
        for k in range(8):
            peer = (k * 2 + zi // 2, (4 * zh + x) * 4 + y)

            @pl.when(jnp.logical_not(is_me(peer)))
            def _():
                greet(peer)

    final_from = [((zl // 4) * 8 + zi * 2 + c, (x + 4 * g) * 4 + y) for g in (0, 1)]
    final_to = [(h * 8 + zi * 2 + c, (4 * zh + x) * 4 + y) for h in (0, 1)]
    count = len(sym)
    for peer in final_from:
        @pl.when(jnp.logical_not(is_me(peer)))
        def _():
            greet(peer)
    for peer in heads + final_to:
        count = count + 1 - b2i(is_me(peer))
    time_ref[...] = jnp.broadcast_to(
        jnp.transpose((jnp.broadcast_to(step_ref[...], (8, 64)).astype(F32) + 0.5) / NBINS)[:, 0:1], (64, 512)
    )
    load_noise.wait()
    pl.semaphore_wait(barrier, count)

    def first(g):
        return remote(noise_ref, buf.at[head_h, q_me], first_send.at[g], arrive.at[head_h, q_me], heads[g])

    for g in (0, 1):
        @pl.when(jnp.logical_not(is_me(heads[g])))
        def _():
            first(g).start()

        @pl.when(is_me(heads[g]))
        def _():
            pltpu.make_async_copy(noise_ref, buf.at[head_h, q_me], arrive.at[head_h, q_me]).start()

    load_data.wait()
    dsq_ref[...] = jnp.broadcast_to(
        jnp.sum(jnp.square(data_ref[...].astype(F32)), axis=1, keepdims=True), (256, 128)
    )

    def landed(h, q):
        pltpu.make_async_copy(noise_ref, buf.at[h, q], arrive.at[h, q]).wait()

    def hop(h, q, kind, peer):
        return remote(buf.at[h, q], buf.at[h, q], send.at[h, q, kind], arrive.at[h, q], peer)

    near = zi // 2

    def side(k):
        return near if k == 0 else 1 - near

    def around(h):
        return lax.rem(y - (2 * c + h) + 4, 4)

    def forwards(h, q, act):
        r = around(h)
        j, upward = q % 8, q < 8
        on_chain = r == 0

        inner = jnp.logical_or(zi == 1, zi == 2)

        @pl.when(on_chain & jnp.where(upward, inner, zi == 2))
        def _():
            act(hop(h, q, 0, zup))

        @pl.when(on_chain & jnp.where(upward, zi == 1, inner))
        def _():
            act(hop(h, q, 4, zdown))

        straight = jnp.where(upward == (near == 0), DIRECT[0], DIRECT[1])
        relay = jnp.logical_not(straight)

        @pl.when(jnp.logical_or(on_chain, jnp.logical_and(relay, jnp.logical_and(r == 1, j % 2 == 0))))
        def _():
            act(hop(h, q, 1, yup))

        @pl.when(jnp.logical_or(on_chain, jnp.logical_and(relay, jnp.logical_and(r == 3, j % 2 == 1))))
        def _():
            act(hop(h, q, 2, ydown))

        @pl.when(jnp.logical_and(on_chain, straight))
        def _():
            act(hop(h, q, 3, ypeers[1]))

    def waits_early(r, k):
        return jnp.logical_and(jnp.logical_or(r == 1, r == 3), not DIRECT[k])

    def tick(t, carry):
        for lagging in (0, 1):
            for h in (0, 1):
                r = around(h)
                s = t - LAG * lagging
                mine = r == 0
                if lagging == 1:
                    mine = jnp.logical_and(waits_early(r, 0), s < 8) | jnp.logical_and(waits_early(r, 1), s >= 8)

                @pl.when(jnp.logical_and(mine, jnp.logical_and(s >= 0, s < 16)))
                def _():
                    q = 8 * jnp.where(s < 8, near, 1 - near) + s % 8
                    landed(h, q)
                    forwards(h, q, lambda cp: cp.start())
        return carry

    def last_columns(k, lo, hi):
        def body(j, carry):
            for h in (0, 1):
                r = around(h)

                @pl.when(jnp.logical_not(jnp.logical_or(r == 0, waits_early(r, k))))
                def _():
                    landed(h, 8 * side(k) + j)
            return carry

        lax.fori_loop(lo, hi, body, 0)


    blocks = (4, 2, 2)
    offset = (0, 4, 6)
    base = (4 * near, 4 - 4 * near, 6 - 4 * near)

    def costs(k):
        def pair(b, carry):
            at = base[k] + 2 * b
            acc = jnp.concatenate([dsq_ref[...]] * 2, axis=1)
            sq = jnp.zeros((256, 128), F32)
            for h in (0, 1):
                piece = buf[h, pl.ds(2 * at, 4)].reshape(256, 512)
                acc -= 2.0 * lax.dot_general(
                    data_ref[:, 512 * h:512 * (h + 1)], piece, (((1,), (1,)), ((), ())), preferred_element_type=F32
                )
                for i in range(4):
                    wide = piece[:, 128 * i:128 * (i + 1)].astype(F32)
                    sq += wide * wide
            nsq = jnp.sum(jnp.transpose(sq), axis=0, keepdims=True)
            acc = (acc + nsq) * scale
            part[offset[k] + 2 * b] = acc[:, 0:128]
            part[offset[k] + 2 * b + 1] = acc[:, 128:256]
            return carry

        lax.fori_loop(0, blocks[k] // 2, pair, 0)

    def chunk(k):
        return pl.ds(offset[k], blocks[k])

    def core_sum(k):
        return remote(
            part.at[chunk(k), pl.ds(128 * (1 - c), 128)], half.at[chunk(k)], c_send.at[k], c_recv.at[k], other
        )

    def core_done(k):
        core_sum(k).wait()
        half[chunk(k)] = half[chunk(k)] + part[chunk(k), pl.ds(pl.multiple_of(128 * c, 128), 128)]

    def x_sum(k, i, slot):
        return remote(
            half.at[chunk(k), pl.ds(32 * xq(i), 32)], xin.at[slot, chunk(k)],
            x_send.at[k, i], x_recv.at[k, slot], xpeers[i - 1],
        )

    def x_start(k):
        for i in (1, 2, 3):
            x_sum(k, i, x).start()

    def z_sum(k):
        return remote(own.at[chunk(k)], zin.at[chunk(k)], z_send.at[k], z_recv.at[k], far)

    def x_done(k):
        acc = half[chunk(k), pl.ds(pl.multiple_of(32 * x, 32), 32)]
        for i in (1, 2, 3):
            x_sum(k, i, xq(i)).wait()
            acc += xin[xq(i), chunk(k)]
        own[chunk(k)] = acc
        z_sum(k).start()

    def slab(k, cc, xx):
        return s_ref.at[pl.ds(base[k], blocks[k]), pl.ds(128 * cc + 32 * xx, 32)]

    def z_done(k):
        z_sum(k).wait()
        mine = pl.ds(pl.multiple_of(128 * c + 32 * x, 32), 32)
        s_ref[pl.ds(base[k], blocks[k]), mine] = own[chunk(k)] + zin[chunk(k)]
        for i in (1, 2, 3):
            remote(slab(k, c, x), slab(k, c, x), gx_send.at[k, i], gx_recv.at[k, x], xpeers[i - 1]).start()

    def core_gather(k, cc):
        place = s_ref.at[pl.ds(base[k], blocks[k]), pl.ds(128 * cc, 128)]
        return remote(place, place, gc_send.at[k], gc_recv.at[k], other)

    def gx_done(k):
        for i in (1, 2, 3):
            remote(slab(k, c, x), slab(k, c, xq(i)), gx_send.at[k, i], gx_recv.at[k, xq(i)], xpeers[i - 1]).wait()
        core_gather(k, c).start()

    def gc_done(k):
        core_gather(k, c).wait_send()
        core_gather(k, 1 - c).wait_recv()

    srcc = y // 2

    def spread(act):
        for h in (0, 1):
            for cc in (0, 1):
                same = jnp.logical_and(c == cc, y == 2 * c + h)
                src = data_ref.at[:, pl.ds(512 * h, 512)]

                @pl.when(jnp.logical_not(same))
                def _():
                    peer = (zh * 8 + x * 2 + cc, zl * 4 + 2 * c + h)
                    act(remote(src, dt_ref.at[y], as_.at[h, cc], ar.at[y], peer), False)

                @pl.when(same)
                def _():
                    act(pltpu.make_async_copy(src, dt_ref.at[y], loc), True)

    lax.fori_loop(0, 8 + LAG, tick, 0)
    last_columns(0, 0, 8)
    costs(0)
    core_sum(0).start()
    lax.fori_loop(8 + LAG, 12 + LAG, tick, 0)
    core_done(0)
    x_start(0)
    last_columns(1, 0, 4)
    costs(1)
    core_sum(1).start()
    lax.fori_loop(12 + LAG, 16 + LAG, tick, 0)
    x_done(0)
    core_done(1)
    x_start(1)
    last_columns(1, 4, 8)
    costs(2)
    core_sum(2).start()
    x_done(1)
    core_done(2)
    x_start(2)
    spread(lambda cp, local: cp.start())
    x_done(2)
    z_done(0)
    gx_done(0)
    z_done(1)
    gx_done(1)
    z_done(2)
    gx_done(2)
    for k in range(3):
        gc_done(k)

    def lse0(v):
        m = jnp.max(v, axis=0)
        return m + jnp.log2(jnp.sum(jnp.exp2(v - m[None]), axis=0))

    def z_rows(k):
        for i, peer in enumerate(zpeers):
            remote(row.at[k], rz.at[k, zl], zs.at[k, i], zr.at[k, zl], peer).start()
        rz[k, zl] = row[k]

    def all_rows(k, total):
        for i, peer in enumerate(zpeers):
            remote(row.at[k], rz.at[k, zq(i + 1)], zs.at[k, i], zr.at[k, zq(i + 1)], peer).wait()
        ry[k, y] = total(rz[k])
        mine = ry.at[k, y]
        for i, peer in enumerate(ypeers):
            remote(mine, mine, ys.at[k, i], yr.at[k, y], peer).start()
        for i, peer in enumerate(ypeers):
            remote(mine, ry.at[k, yq(i + 1)], ys.at[k, i], yr.at[k, yq(i + 1)], peer).wait()
        return total(ry[k])

    for b in range(8):
        v = -s_ref[b]
        m = jnp.max(v, axis=0, keepdims=True)
        row[0, b:b + 1, :] = m + jnp.log2(jnp.sum(jnp.exp2(v - m), axis=0, keepdims=True))
    z_rows(0)
    f = -all_rows(0, lse0)
    fpot[...] = f
    m = f[0:1] - s_ref[0]
    for b in range(1, 8):
        m = jnp.maximum(m, f[b:b + 1] - s_ref[b])
    m = jnp.broadcast_to(jnp.max(m, axis=1, keepdims=True), (256, 128))
    tot = jnp.zeros((256, 128), F32)
    for b in range(8):
        tot += jnp.exp2(f[b:b + 1] - s_ref[b] - m)
    gpot[...] = -(m + jnp.log2(jnp.broadcast_to(jnp.sum(tot, axis=1, keepdims=True), (256, 128))))

    def add0(v):
        return jnp.sum(v, axis=0)

    def iteration(k, carry):
        g = gpot[...]
        f = fpot[...]
        for b in range(8):
            row[k, b:b + 1, :] = jnp.sum(jnp.exp2(g - s_ref[b] + f[b:b + 1]), axis=0, keepdims=True)
        z_rows(k)
        f = f - jnp.log2(all_rows(k, add0))
        fpot[...] = f
        tot = jnp.zeros((256, 128), F32)
        for b in range(8):
            tot += jnp.exp2(g - s_ref[b] + f[b:b + 1])
        gpot[...] = g - jnp.log2(jnp.broadcast_to(jnp.sum(tot, axis=1, keepdims=True), (256, 128)))
        return carry

    lax.fori_loop(1, ITERS, iteration, 0)

    g = gpot[...]
    f = fpot[...]
    for b in (0, 1, 4, 5, 2, 3, 6, 7):
        e = jnp.exp2(g - s_ref[b] + f[b:b + 1])
        w_ref[b] = e.astype(BF16)
        row[ITERS, b:b + 1, :] = jnp.sum(e, axis=0, keepdims=True)

    def wsend(b, k, peer):
        return remote(w_ref.at[4 * c + b], wbuf.at[y, b], ws.at[k, b], wr.at[y, b], peer)

    def wpass(b, src, k, peer):
        return remote(wbuf.at[src, b], wbuf.at[src, b], ws.at[k, b], wr.at[src, b], peer)

    def wwait(b, src):
        remote(w_ref.at[b], wbuf.at[src, b], ws.at[0, b], wr.at[src, b], yup).wait_recv()

    left, right, opposite = yq(3), yq(1), yq(2)
    for b in range(4):
        wsend(b, 0, yup).start()
        wsend(b, 1, ydown).start()
    z_rows(ITERS)
    wbuf[y] = w_ref[pl.ds(4 * c, 4)]
    spread(lambda cp, local: cp.wait() if local else cp.wait_send())
    for k in range(4):
        @pl.when(jnp.logical_not(jnp.logical_and(srcc == c, y == k)))
        def _():
            peer = (zh * 8 + x * 2 + srcc, zl * 4 + k)
            remote(dt_ref.at[k], dt_ref.at[k], as_.at[0, 0], ar.at[k], peer).wait_recv()

    def wforward(b):
        if b % 2 == 0:
            wwait(b, left)
            wpass(b, left, 2, yup).start()
        else:
            wwait(b, right)
            wpass(b, right, 2, ydown).start()

    def quad(i):
        return (n, (4 * zg + (zi + i) % 4) * 4 + y)

    def quad_sum(h, i, slot):
        return remote(stage.at[h, (zi + i) % 4], qin.at[h, slot], qs.at[h, i], qr.at[h, slot], quad(i))

    wforward(0)
    wforward(1)
    for h in (0, 1):
        for bb in (0, 1):
            b = 2 * h + bb
            wwait(b, right if b % 2 == 0 else left)
            wwait(b, opposite)
            acc = jnp.zeros((128, 512), F32)
            for k in range(4):
                acc += lax.dot_general(
                    wbuf[k, b], dt_ref[k], (((0,), (0,)), ((), ())), preferred_element_type=F32
                )
            tpart[h, 2 * bb:2 * bb + 2] = acc.reshape(2, 64, 512)
            stage[h, 2 * bb:2 * bb + 2] = acc.reshape(2, 64, 512).astype(BF16)
        for i in (1, 2, 3):
            quad_sum(h, i, zi).start()
        if h == 0:
            wforward(2)
            wforward(3)

    def final(h):
        return remote(fin.at[h], got.at[zg], fs.at[h], fr.at[zg], final_to[h])

    for h in (0, 1):
        acc = tpart[h, zi]
        for i in (1, 2, 3):
            quad_sum(h, i, (zi + i) % 4).wait()
            acc += qin[h, (zi + i) % 4].astype(F32)
        fin[h] = acc.astype(BF16)

        @pl.when(jnp.logical_not(is_me(final_to[h])))
        def _():
            final(h).start()

        @pl.when(is_me(final_to[h]))
        def _():
            pltpu.make_async_copy(fin.at[h], got.at[zg], fr.at[zg]).start()

    total = 1.0 / all_rows(ITERS, add0)
    columns = jnp.transpose(total)
    mine_b = 4 * c + 2 * zh + x // 2
    picked = jnp.zeros((128, 1), F32)
    for b in range(8):
        picked = jnp.where(mine_b == b, columns[:, b:b + 1], picked)
    picked = jnp.where(x % 2 == 0, picked[0:64], picked[64:128])

    for g in (0, 1):
        @pl.when(jnp.logical_not(is_me(heads[g])))
        def _():
            first(g).wait_send()

    def drain(q, carry):
        for h in (0, 1):
            forwards(h, q, lambda cp: cp.wait_send())
        return carry

    lax.fori_loop(0, 16, drain, 0)
    for b in range(4):
        wsend(b, 0, yup).wait_send()
        wsend(b, 1, ydown).wait_send()
        if b % 2 == 0:
            wpass(b, left, 2, yup).wait_send()
        else:
            wpass(b, right, 2, ydown).wait_send()
    for g in (0, 1):
        pltpu.make_async_copy(fin.at[0], got.at[g], fr.at[g]).wait()
    out_ref[...] = (got[0].astype(F32) + got[1].astype(F32)) * picked
    for h in (0, 1):
        @pl.when(jnp.logical_not(is_me(final_to[h])))
        def _():
            final(h).wait_send()


DMA = pltpu.SemaphoreType.DMA


def fused_call(noise, data, timestep):
    scale = LOG2E / (16384.0 * EPS)
    rounds = ITERS + 1
    return pl.pallas_call(
        functools.partial(fused_kernel, scale),
        out_shape=[jax.ShapeDtypeStruct((64, 512), F32), jax.ShapeDtypeStruct((64, 512), F32)],
        in_specs=[pl.BlockSpec(memory_space=pl.ANY)] * 2 + [pl.BlockSpec(memory_space=VMEM)],
        out_specs=[pl.BlockSpec(memory_space=VMEM)] * 2,
        scratch_shapes=[
            VMEM((64, 512), BF16), VMEM((256, 1024), BF16), VMEM((256, 128), F32),
            VMEM((2, 16, 64, 512), BF16),
            VMEM((8, 256, 128), F32), VMEM((8, 128, 128), F32), VMEM((4, 8, 32, 128), F32),
            VMEM((8, 32, 128), F32), VMEM((8, 32, 128), F32), VMEM((8, 256, 128), F32),
            VMEM((256, 128), F32), VMEM((8, 128), F32), VMEM((rounds, 8, 128), F32), VMEM((rounds, 8, 8, 128), F32),
            VMEM((rounds, 4, 8, 128), F32),
            VMEM((8, 256, 128), BF16), VMEM((4, 256, 512), BF16), VMEM((4, 4, 256, 128), BF16),
            VMEM((2, 4, 64, 512), F32), VMEM((2, 4, 64, 512), BF16), VMEM((2, 4, 64, 512), BF16),
            VMEM((2, 64, 512), BF16), VMEM((2, 64, 512), BF16),
            DMA((2,)), DMA((2,)), DMA((2, 16)), DMA((2, 16, 5)),
            DMA((3,)), DMA((3,)), DMA((3, 4)), DMA((3, 4)), DMA((3,)), DMA((3,)),
            DMA((3, 4)), DMA((3, 4)), DMA((3,)), DMA((3,)),
            DMA((rounds, 7)), DMA((rounds, 8)), DMA((rounds, 3)), DMA((rounds, 4)),
            DMA((2, 2)), DMA((4,)), DMA, DMA((3, 4)), DMA((4, 4)),
            DMA((2, 4)), DMA((2, 4)), DMA((2,)), DMA((2,)),
        ],
        compiler_params=pltpu.CompilerParams(
            collective_id=1, has_side_effects=True, vmem_limit_bytes=62 * 1024 * 1024
        ),
    )(noise, data, timestep)


def per_device(noise, data, timestep):
    targets, t_wide = fused_call(noise, data, timestep.reshape(1, 64))
    noise_f = noise.astype(F32)
    t_val = t_wide
    inputs_t = ((1.0 - t_val) * noise_f + t_val * targets).astype(BF16)
    velocity = (targets - noise_f).astype(BF16)
    return (inputs_t, velocity)


def solution(mesh):
    placed = (P("noise", "dp"), P("dp", "noise"), P("noise"))
    return jax.shard_map(
        per_device,
        mesh=mesh,
        in_specs=placed,
        out_specs=(P("noise", "dp"), P("noise", "dp")),
        check_vma=False,
    )
```

```python
import functools

import jax
import jax.numpy as jnp
from jax import lax
from jax.experimental import pallas as pl
from jax.experimental.pallas import tpu as pltpu
from jax.sharding import PartitionSpec as P

ITERS = 4
NBINS = 1000
EPS = 0.002
LOG2E = 1.4426950408889634
MESH = pl.DeviceIdType.MESH
VMEM = pltpu.VMEM
F32 = jnp.float32
BF16 = jnp.bfloat16
LAG = 4
DIRECT = (True, False)


def remote(src, dst, send, recv, peer):
    return pltpu.make_async_remote_copy(
        src_ref=src, dst_ref=dst, send_sem=send, recv_sem=recv, device_id=peer, device_id_type=MESH
    )


def b2i(cond):
    return jnp.where(cond, 1, 0).astype(jnp.int32)


def fused_kernel(scale, noise_hbm, data_hbm, step_ref, out_ref, time_ref,
                 noise_ref, data_ref, dsq_ref, buf, part, half, xin, own, zin, s_ref,
                 gpot, fpot, pin, cin, row, rz, ry, w_ref, dt_ref, wbuf, tpart, stage, qin, fin, got,
                 load_sem, first_send, arrive, send,
                 c_send, c_recv, x_send, x_recv, z_send, z_recv, gx_send, gx_recv, gc_send, gc_recv,
                 ps, pr, cs, cr, zs, zr, ys, yr, as_, ar, loc, ws, wr, qs, qr, fs, fr):
    n, d = lax.axis_index("noise"), lax.axis_index("dp")
    zh, x, c, zl, y = n // 8, (n // 2) % 4, n % 2, d // 4, d % 4
    load_noise = pltpu.make_async_copy(noise_hbm, noise_ref, load_sem.at[0])
    load_data = pltpu.make_async_copy(data_hbm, data_ref, load_sem.at[1])
    load_noise.start()
    load_data.start()

    other_n = n + 1 - 2 * c
    other = (other_n, d)
    far = (lax.rem(n + 8, 16), d)

    def xq(k):
        return lax.rem(x + k, 4)

    def yq(k):
        return lax.rem(y + k, 4)

    def zq(k):
        return lax.rem(zl + k, 8)

    xpeers = [(zh * 8 + xq(k) * 2 + c, d) for k in (1, 2, 3)]
    ypeers = [(n, zl * 4 + yq(k)) for k in (1, 2, 3)]
    zpeers = [(n, zq(k) * 4 + y) for k in range(1, 8)]
    yup, ydown = ypeers[0], ypeers[2]
    across = [(other_n, zl * 4 + yq(k)) for k in (1, 2, 3)]
    zup, zdown = zpeers[0], zpeers[6]
    shifts = [(i, j) for i in range(4) for j in range(4) if i + j > 0]
    plane = [(zh * 8 + xq(i) * 2 + c, zl * 4 + yq(j)) for i, j in shifts]
    corners = [peer for peer, (i, j) in zip(plane, shifts) if i > 0 and j > 0]
    zi, zg = zl % 4, zl // 4

    head_n, head_h = d // 2, y % 2
    heads = [(head_n, (4 * g + 1 + c) * 4 + y) for g in (0, 1)]
    q_me = c * 8 + zh * 4 + x

    def is_me(peer):
        return jnp.logical_and(peer[0] == n, peer[1] == d)

    barrier = pltpu.get_barrier_semaphore()

    def greet(peer):
        pl.semaphore_signal(barrier, inc=1, device_id=peer, device_id_type=MESH)

    sym = [other, far] + xpeers + ypeers + zpeers + across + corners
    for peer in sym:
        greet(peer)
    is_head = jnp.logical_and(c == y // 2, jnp.logical_or(zi == 1, zi == 2))

    @pl.when(is_head)
    def _():
        for k in range(8):
            peer = (k * 2 + zi // 2, (4 * zh + x) * 4 + y)

            @pl.when(jnp.logical_not(is_me(peer)))
            def _():
                greet(peer)

    final_from = [((zl // 4) * 8 + zi * 2 + c, (x + 4 * g) * 4 + y) for g in (0, 1)]
    final_to = [(h * 8 + zi * 2 + c, (4 * zh + x) * 4 + y) for h in (0, 1)]
    count = len(sym)
    for peer in final_from:
        @pl.when(jnp.logical_not(is_me(peer)))
        def _():
            greet(peer)
    for peer in heads + final_to:
        count = count + 1 - b2i(is_me(peer))
    time_ref[...] = jnp.broadcast_to(
        jnp.transpose((jnp.broadcast_to(step_ref[...], (8, 64)).astype(F32) + 0.5) / NBINS)[:, 0:1], (64, 512)
    )
    load_noise.wait()
    pl.semaphore_wait(barrier, count)

    def first(g):
        return remote(noise_ref, buf.at[head_h, q_me], first_send.at[g], arrive.at[head_h, q_me], heads[g])

    for g in (0, 1):
        @pl.when(jnp.logical_not(is_me(heads[g])))
        def _():
            first(g).start()

        @pl.when(is_me(heads[g]))
        def _():
            pltpu.make_async_copy(noise_ref, buf.at[head_h, q_me], arrive.at[head_h, q_me]).start()

    load_data.wait()
    dsq_ref[...] = jnp.broadcast_to(
        jnp.sum(jnp.square(data_ref[...].astype(F32)), axis=1, keepdims=True), (256, 128)
    )

    def landed(h, q):
        pltpu.make_async_copy(noise_ref, buf.at[h, q], arrive.at[h, q]).wait()

    def hop(h, q, kind, peer):
        return remote(buf.at[h, q], buf.at[h, q], send.at[h, q, kind], arrive.at[h, q], peer)

    near = zi // 2

    def side(k):
        return near if k == 0 else 1 - near

    def around(h):
        return lax.rem(y - (2 * c + h) + 4, 4)

    def forwards(h, q, act):
        r = around(h)
        j, upward = q % 8, q < 8
        on_chain = r == 0

        inner = jnp.logical_or(zi == 1, zi == 2)

        @pl.when(on_chain & jnp.where(upward, inner, zi == 2))
        def _():
            act(hop(h, q, 0, zup))

        @pl.when(on_chain & jnp.where(upward, zi == 1, inner))
        def _():
            act(hop(h, q, 4, zdown))

        straight = jnp.where(upward == (near == 0), DIRECT[0], DIRECT[1])
        relay = jnp.logical_not(straight)

        @pl.when(jnp.logical_or(on_chain, jnp.logical_and(relay, jnp.logical_and(r == 1, j % 2 == 0))))
        def _():
            act(hop(h, q, 1, yup))

        @pl.when(jnp.logical_or(on_chain, jnp.logical_and(relay, jnp.logical_and(r == 3, j % 2 == 1))))
        def _():
            act(hop(h, q, 2, ydown))

        @pl.when(jnp.logical_and(on_chain, straight))
        def _():
            act(hop(h, q, 3, ypeers[1]))

    def waits_early(r, k):
        return jnp.logical_and(jnp.logical_or(r == 1, r == 3), not DIRECT[k])

    def tick(t, carry):
        for lagging in (0, 1):
            for h in (0, 1):
                r = around(h)
                s = t - LAG * lagging
                mine = r == 0
                if lagging == 1:
                    mine = jnp.logical_and(waits_early(r, 0), s < 8) | jnp.logical_and(waits_early(r, 1), s >= 8)

                @pl.when(jnp.logical_and(mine, jnp.logical_and(s >= 0, s < 16)))
                def _():
                    q = 8 * jnp.where(s < 8, near, 1 - near) + s % 8
                    landed(h, q)
                    forwards(h, q, lambda cp: cp.start())
        return carry

    def last_columns(k, lo, hi):
        def body(j, carry):
            for h in (0, 1):
                r = around(h)

                @pl.when(jnp.logical_not(jnp.logical_or(r == 0, waits_early(r, k))))
                def _():
                    landed(h, 8 * side(k) + j)
            return carry

        lax.fori_loop(lo, hi, body, 0)


    blocks = (4, 2, 2)
    offset = (0, 4, 6)
    base = (4 * near, 4 - 4 * near, 6 - 4 * near)

    def costs(k):
        def pair(b, carry):
            at = base[k] + 2 * b
            acc = jnp.concatenate([dsq_ref[...]] * 2, axis=1)
            sq = jnp.zeros((256, 128), F32)
            for h in (0, 1):
                piece = buf[h, pl.ds(2 * at, 4)].reshape(256, 512)
                acc -= 2.0 * lax.dot_general(
                    data_ref[:, 512 * h:512 * (h + 1)], piece, (((1,), (1,)), ((), ())), preferred_element_type=F32
                )
                for i in range(4):
                    wide = piece[:, 128 * i:128 * (i + 1)].astype(F32)
                    sq += wide * wide
            nsq = jnp.sum(jnp.transpose(sq), axis=0, keepdims=True)
            acc = (acc + nsq) * scale
            part[offset[k] + 2 * b] = acc[:, 0:128]
            part[offset[k] + 2 * b + 1] = acc[:, 128:256]
            return carry

        lax.fori_loop(0, blocks[k] // 2, pair, 0)

    def chunk(k):
        return pl.ds(offset[k], blocks[k])

    def core_sum(k):
        return remote(
            part.at[chunk(k), pl.ds(128 * (1 - c), 128)], half.at[chunk(k)], c_send.at[k], c_recv.at[k], other
        )

    def core_done(k):
        core_sum(k).wait()
        half[chunk(k)] = half[chunk(k)] + part[chunk(k), pl.ds(pl.multiple_of(128 * c, 128), 128)]

    def x_sum(k, i, slot):
        return remote(
            half.at[chunk(k), pl.ds(32 * xq(i), 32)], xin.at[slot, chunk(k)],
            x_send.at[k, i], x_recv.at[k, slot], xpeers[i - 1],
        )

    def x_start(k):
        for i in (1, 2, 3):
            x_sum(k, i, x).start()

    def z_sum(k):
        return remote(own.at[chunk(k)], zin.at[chunk(k)], z_send.at[k], z_recv.at[k], far)

    def x_done(k):
        acc = half[chunk(k), pl.ds(pl.multiple_of(32 * x, 32), 32)]
        for i in (1, 2, 3):
            x_sum(k, i, xq(i)).wait()
            acc += xin[xq(i), chunk(k)]
        own[chunk(k)] = acc
        z_sum(k).start()

    def slab(k, cc, xx):
        return s_ref.at[pl.ds(base[k], blocks[k]), pl.ds(128 * cc + 32 * xx, 32)]

    def z_done(k):
        z_sum(k).wait()
        mine = pl.ds(pl.multiple_of(128 * c + 32 * x, 32), 32)
        s_ref[pl.ds(base[k], blocks[k]), mine] = own[chunk(k)] + zin[chunk(k)]
        for i in (1, 2, 3):
            remote(slab(k, c, x), slab(k, c, x), gx_send.at[k, i], gx_recv.at[k, x], xpeers[i - 1]).start()

    def core_gather(k, cc):
        place = s_ref.at[pl.ds(base[k], blocks[k]), pl.ds(128 * cc, 128)]
        return remote(place, place, gc_send.at[k], gc_recv.at[k], other)

    def gx_done(k):
        for i in (1, 2, 3):
            remote(slab(k, c, x), slab(k, c, xq(i)), gx_send.at[k, i], gx_recv.at[k, xq(i)], xpeers[i - 1]).wait()
        core_gather(k, c).start()

    def gc_done(k):
        core_gather(k, c).wait_send()
        core_gather(k, 1 - c).wait_recv()

    srcc = y // 2

    def spread(act):
        for h in (0, 1):
            for cc in (0, 1):
                same = jnp.logical_and(c == cc, y == 2 * c + h)
                src = data_ref.at[:, pl.ds(512 * h, 512)]

                @pl.when(jnp.logical_not(same))
                def _():
                    peer = (zh * 8 + x * 2 + cc, zl * 4 + 2 * c + h)
                    act(remote(src, dt_ref.at[y], as_.at[h, cc], ar.at[y], peer), False)

                @pl.when(same)
                def _():
                    act(pltpu.make_async_copy(src, dt_ref.at[y], loc), True)

    lax.fori_loop(0, 8 + LAG, tick, 0)
    last_columns(0, 0, 8)
    costs(0)
    core_sum(0).start()
    lax.fori_loop(8 + LAG, 12 + LAG, tick, 0)
    core_done(0)
    x_start(0)
    last_columns(1, 0, 4)
    costs(1)
    core_sum(1).start()
    lax.fori_loop(12 + LAG, 16 + LAG, tick, 0)
    x_done(0)
    core_done(1)
    x_start(1)
    last_columns(1, 4, 8)
    costs(2)
    core_sum(2).start()
    x_done(1)
    core_done(2)
    x_start(2)
    spread(lambda cp, local: cp.start())
    x_done(2)
    z_done(0)
    gx_done(0)
    z_done(1)
    gx_done(1)
    def lse0(v):
        m = jnp.max(v, axis=0)
        return m + jnp.log2(jnp.sum(jnp.exp2(v - m[None]), axis=0))

    def z_rows(k):
        for i, peer in enumerate(zpeers):
            remote(row.at[k], rz.at[k, zl], zs.at[k, i], zr.at[k, zl], peer).start()
        rz[k, zl] = row[k]

    z_done(2)
    v = -s_ref[:, pl.ds(pl.multiple_of(128 * c + 32 * x, 32), 32)]
    m = jnp.max(v, axis=1)
    row[0] = m + jnp.log2(jnp.sum(jnp.exp2(v - m[:, None]), axis=1))
    z_rows(0)
    gx_done(2)
    for k in range(3):
        gc_done(k)

    def all_rows(k, total):
        for i, peer in enumerate(zpeers):
            remote(row.at[k], rz.at[k, zq(i + 1)], zs.at[k, i], zr.at[k, zq(i + 1)], peer).wait()
        ry[k, y] = total(rz[k])
        mine = ry.at[k, y]
        for i, peer in enumerate(ypeers):
            remote(mine, mine, ys.at[k, i], yr.at[k, y], peer).start()
        for i, peer in enumerate(ypeers):
            remote(mine, ry.at[k, yq(i + 1)], ys.at[k, i], yr.at[k, yq(i + 1)], peer).wait()
        return total(ry[k])

    for i, peer in enumerate(zpeers):
        remote(row.at[0], rz.at[0, zq(i + 1)], zs.at[0, i], zr.at[0, zq(i + 1)], peer).wait()
    spot = 4 * x + y
    pin[spot] = lse0(rz[0])
    for i, peer in enumerate(plane):
        remote(pin.at[spot], pin.at[spot], ps.at[i], pr.at[spot], peer).start()
    for i, peer in enumerate(plane):
        there = 4 * xq(shifts[i][0]) + yq(shifts[i][1])
        remote(pin.at[spot], pin.at[there], ps.at[i], pr.at[there], peer).wait()
    cin[c] = lse0(pin[...])
    remote(cin.at[c], cin.at[c], cs.at[0], cr.at[c], other).start()
    remote(cin.at[c], cin.at[1 - c], cs.at[0], cr.at[1 - c], other).wait()
    f = -lse0(cin[...])
    fpot[...] = f
    m = f[0:1] - s_ref[0]
    for b in range(1, 8):
        m = jnp.maximum(m, f[b:b + 1] - s_ref[b])
    m = jnp.broadcast_to(jnp.max(m, axis=1, keepdims=True), (256, 128))
    tot = jnp.zeros((256, 128), F32)
    for b in range(8):
        tot += jnp.exp2(f[b:b + 1] - s_ref[b] - m)
    gpot[...] = -(m + jnp.log2(jnp.broadcast_to(jnp.sum(tot, axis=1, keepdims=True), (256, 128))))

    def add0(v):
        return jnp.sum(v, axis=0)

    def iteration(k, carry):
        g = gpot[...]
        f = fpot[...]
        for b in range(8):
            row[k, b:b + 1, :] = jnp.sum(jnp.exp2(g - s_ref[b] + f[b:b + 1]), axis=0, keepdims=True)
        z_rows(k)
        f = f - jnp.log2(all_rows(k, add0))
        fpot[...] = f
        tot = jnp.zeros((256, 128), F32)
        for b in range(8):
            tot += jnp.exp2(g - s_ref[b] + f[b:b + 1])
        gpot[...] = g - jnp.log2(jnp.broadcast_to(jnp.sum(tot, axis=1, keepdims=True), (256, 128)))
        return carry

    lax.fori_loop(1, ITERS, iteration, 0)

    def wsend(b, k, peer):
        return remote(w_ref.at[4 * c + b], wbuf.at[y, b], ws.at[k, b], wr.at[y, b], peer)

    def wpass(b, src, k, peer):
        return remote(wbuf.at[src, b], wbuf.at[src, b], ws.at[k, b], wr.at[src, b], peer)

    def wwait(b, src):
        remote(w_ref.at[b], wbuf.at[src, b], ws.at[0, b], wr.at[src, b], yup).wait_recv()

    left, right, opposite = yq(3), yq(1), yq(2)
    g = gpot[...]
    row[ITERS] = jnp.zeros((8, 128), F32)
    for b in range(4):
        e = jnp.exp2(g - s_ref[4 * c + b] + fpot[pl.ds(4 * c + b, 1), :])
        w_ref[4 * c + b] = e.astype(BF16)
        wsend(b, 0, yup).start()
        wsend(b, 1, ydown).start()
        wbuf[y, b] = e.astype(BF16)
        row[ITERS, b:b + 1, :] = jnp.sum(e, axis=0, keepdims=True)
    z_rows(ITERS)
    spread(lambda cp, local: cp.wait() if local else cp.wait_send())
    for k in range(4):
        @pl.when(jnp.logical_not(jnp.logical_and(srcc == c, y == k)))
        def _():
            peer = (zh * 8 + x * 2 + srcc, zl * 4 + k)
            remote(dt_ref.at[k], dt_ref.at[k], as_.at[0, 0], ar.at[k], peer).wait_recv()

    def wforward(b):
        if b % 2 == 0:
            wwait(b, left)
            wpass(b, left, 2, yup).start()
        else:
            wwait(b, right)
            wpass(b, right, 2, ydown).start()

    def quad(i):
        return (n, (4 * zg + (zi + i) % 4) * 4 + y)

    def quad_sum(h, i, slot):
        return remote(stage.at[h, (zi + i) % 4], qin.at[h, slot], qs.at[h, i], qr.at[h, slot], quad(i))

    def mul(b, k):
        prod = lax.dot_general(wbuf[k, b], dt_ref[k], (((0,), (0,)), ((), ())), preferred_element_type=F32)
        return prod.reshape(2, 64, 512)

    def place(b):
        return b // 2, pl.ds(2 * (b % 2), 2)

    def add(b, k):
        h, at = place(b)
        tpart[h, at] += mul(b, k)

    def finish(b):
        wwait(b, opposite)
        h, at = place(b)
        acc = tpart[h, at] + mul(b, opposite)
        tpart[h, at] = acc
        stage[h, at] = acc.astype(BF16)

    def quad_start(h):
        for i in (1, 2, 3):
            quad_sum(h, i, zi).start()

    for b in range(4):
        h, at = place(b)
        tpart[h, at] = mul(b, y)
    wforward(0)
    wforward(1)
    add(0, left)
    add(1, right)
    wforward(2)
    wforward(3)
    wwait(0, right)
    add(0, right)
    wwait(1, left)
    add(1, left)
    finish(0)
    finish(1)
    quad_start(0)
    add(2, left)
    add(3, right)
    wwait(2, right)
    add(2, right)
    wwait(3, left)
    add(3, left)
    finish(2)
    finish(3)
    quad_start(1)

    def final(h):
        return remote(fin.at[h], got.at[zg], fs.at[h], fr.at[zg], final_to[h])

    for h in (0, 1):
        acc = tpart[h, zi]
        for i in (1, 2, 3):
            quad_sum(h, i, (zi + i) % 4).wait()
            acc += qin[h, (zi + i) % 4].astype(F32)
        fin[h] = acc.astype(BF16)

        @pl.when(jnp.logical_not(is_me(final_to[h])))
        def _():
            final(h).start()

        @pl.when(is_me(final_to[h]))
        def _():
            pltpu.make_async_copy(fin.at[h], got.at[zg], fr.at[zg]).start()

    total = 1.0 / all_rows(ITERS, add0)
    columns = jnp.transpose(total)
    mine_b = 2 * zh + x // 2
    picked = jnp.zeros((128, 1), F32)
    for b in range(4):
        picked = jnp.where(mine_b == b, columns[:, b:b + 1], picked)
    picked = jnp.where(x % 2 == 0, picked[0:64], picked[64:128])

    for g in (0, 1):
        @pl.when(jnp.logical_not(is_me(heads[g])))
        def _():
            first(g).wait_send()

    def drain(q, carry):
        for h in (0, 1):
            forwards(h, q, lambda cp: cp.wait_send())
        return carry

    lax.fori_loop(0, 16, drain, 0)
    for b in range(4):
        wsend(b, 0, yup).wait_send()
        wsend(b, 1, ydown).wait_send()
        if b % 2 == 0:
            wpass(b, left, 2, yup).wait_send()
        else:
            wpass(b, right, 2, ydown).wait_send()
    for g in (0, 1):
        pltpu.make_async_copy(fin.at[0], got.at[g], fr.at[g]).wait()
    out_ref[...] = (got[0].astype(F32) + got[1].astype(F32)) * picked
    for h in (0, 1):
        @pl.when(jnp.logical_not(is_me(final_to[h])))
        def _():
            final(h).wait_send()


DMA = pltpu.SemaphoreType.DMA


def fused_call(noise, data, timestep):
    scale = LOG2E / (16384.0 * EPS)
    rounds = ITERS + 1
    return pl.pallas_call(
        functools.partial(fused_kernel, scale),
        out_shape=[jax.ShapeDtypeStruct((64, 512), F32), jax.ShapeDtypeStruct((64, 512), F32)],
        in_specs=[pl.BlockSpec(memory_space=pl.ANY)] * 2 + [pl.BlockSpec(memory_space=VMEM)],
        out_specs=[pl.BlockSpec(memory_space=VMEM)] * 2,
        scratch_shapes=[
            VMEM((64, 512), BF16), VMEM((256, 1024), BF16), VMEM((256, 128), F32),
            VMEM((2, 16, 64, 512), BF16),
            VMEM((8, 256, 128), F32), VMEM((8, 128, 128), F32), VMEM((4, 8, 32, 128), F32),
            VMEM((8, 32, 128), F32), VMEM((8, 32, 128), F32), VMEM((8, 256, 128), F32),
            VMEM((256, 128), F32), VMEM((8, 128), F32), VMEM((16, 8, 128), F32), VMEM((2, 8, 128), F32), VMEM((rounds, 8, 128), F32), VMEM((rounds, 8, 8, 128), F32),
            VMEM((rounds, 4, 8, 128), F32),
            VMEM((8, 256, 128), BF16), VMEM((4, 256, 512), BF16), VMEM((4, 4, 256, 128), BF16),
            VMEM((2, 4, 64, 512), F32), VMEM((2, 4, 64, 512), BF16), VMEM((2, 4, 64, 512), BF16),
            VMEM((2, 64, 512), BF16), VMEM((2, 64, 512), BF16),
            DMA((2,)), DMA((2,)), DMA((2, 16)), DMA((2, 16, 5)),
            DMA((3,)), DMA((3,)), DMA((3, 4)), DMA((3, 4)), DMA((3,)), DMA((3,)),
            DMA((3, 4)), DMA((3, 4)), DMA((3,)), DMA((3,)),
            DMA((15,)), DMA((16,)), DMA((1,)), DMA((2,)),
            DMA((rounds, 7)), DMA((rounds, 8)), DMA((rounds, 3)), DMA((rounds, 4)),
            DMA((2, 2)), DMA((4,)), DMA, DMA((3, 4)), DMA((4, 4)),
            DMA((2, 4)), DMA((2, 4)), DMA((2,)), DMA((2,)),
        ],
        compiler_params=pltpu.CompilerParams(
            collective_id=1, has_side_effects=True, vmem_limit_bytes=40 * 1024 * 1024
        ),
    )(noise, data, timestep)


def per_device(noise, data, timestep):
    targets, t_wide = fused_call(noise, data, timestep.reshape(1, 64))
    noise_f = noise.astype(F32)
    t_val = t_wide
    inputs_t = ((1.0 - t_val) * noise_f + t_val * targets).astype(BF16)
    velocity = (targets - noise_f).astype(BF16)
    return (inputs_t, velocity)


def solution(mesh):
    placed = (P("noise", "dp"), P("dp", "noise"), P("noise"))
    return jax.shard_map(
        per_device,
        mesh=mesh,
        in_specs=placed,
        out_specs=(P("noise", "dp"), P("noise", "dp")),
        check_vma=False,
    )
```

```python
import functools

import jax
import jax.numpy as jnp
from jax import lax
from jax.experimental import pallas as pl
from jax.experimental.pallas import tpu as pltpu
from jax.sharding import PartitionSpec as P

ITERS = 4
NBINS = 1000
EPS = 0.002
LOG2E = 1.4426950408889634
MESH = pl.DeviceIdType.MESH
VMEM = pltpu.VMEM
F32 = jnp.float32
BF16 = jnp.bfloat16
LAG = 4
DIRECT = (False, False)


def remote(src, dst, send, recv, peer):
    return pltpu.make_async_remote_copy(
        src_ref=src, dst_ref=dst, send_sem=send, recv_sem=recv, device_id=peer, device_id_type=MESH
    )


def b2i(cond):
    return jnp.where(cond, 1, 0).astype(jnp.int32)


def fused_kernel(scale, noise_hbm, data_hbm, step_ref, out_ref, time_ref,
                 noise_ref, data_ref, dsq_ref, buf, part, half, xin, own, zin, s_ref,
                 gpot, fpot, row, rz, ry, w_ref, dt_ref, wbuf, tpart, stage, qin, fin, got,
                 load_sem, first_send, arrive, send,
                 c_send, c_recv, x_send, x_recv, z_send, z_recv, gx_send, gx_recv, gc_send, gc_recv,
                 zs, zr, ys, yr, as_, ar, loc, ws, wr, qs, qr, fs, fr):
    n, d = lax.axis_index("noise"), lax.axis_index("dp")
    zh, x, c, zl, y = n // 8, (n // 2) % 4, n % 2, d // 4, d % 4
    load_noise = pltpu.make_async_copy(noise_hbm, noise_ref, load_sem.at[0])
    load_data = pltpu.make_async_copy(data_hbm, data_ref, load_sem.at[1])
    load_noise.start()
    load_data.start()

    other_n = n + 1 - 2 * c
    other = (other_n, d)
    far = (lax.rem(n + 8, 16), d)

    def xq(k):
        return lax.rem(x + k, 4)

    def yq(k):
        return lax.rem(y + k, 4)

    def zq(k):
        return lax.rem(zl + k, 8)

    xpeers = [(zh * 8 + xq(k) * 2 + c, d) for k in (1, 2, 3)]
    ypeers = [(n, zl * 4 + yq(k)) for k in (1, 2, 3)]
    zpeers = [(n, zq(k) * 4 + y) for k in range(1, 8)]
    yup, ydown = ypeers[0], ypeers[2]
    across = [(other_n, zl * 4 + yq(k)) for k in (1, 2, 3)]
    zup, zdown = zpeers[0], zpeers[6]
    zi, zg = zl % 4, zl // 4

    head_n, head_h = d // 2, y % 2
    heads = [(head_n, (4 * g + 1 + c) * 4 + y) for g in (0, 1)]
    q_me = c * 8 + zh * 4 + x

    def is_me(peer):
        return jnp.logical_and(peer[0] == n, peer[1] == d)

    barrier = pltpu.get_barrier_semaphore()

    def greet(peer):
        pl.semaphore_signal(barrier, inc=1, device_id=peer, device_id_type=MESH)

    sym = [other, far] + xpeers + ypeers + zpeers + across
    for peer in sym:
        greet(peer)
    is_head = jnp.logical_and(c == y // 2, jnp.logical_or(zi == 1, zi == 2))

    @pl.when(is_head)
    def _():
        for k in range(8):
            peer = (k * 2 + zi // 2, (4 * zh + x) * 4 + y)

            @pl.when(jnp.logical_not(is_me(peer)))
            def _():
                greet(peer)

    final_from = [((zl // 4) * 8 + zi * 2 + c, (x + 4 * g) * 4 + y) for g in (0, 1)]
    final_to = [(h * 8 + zi * 2 + c, (4 * zh + x) * 4 + y) for h in (0, 1)]
    count = len(sym)
    for peer in final_from:
        @pl.when(jnp.logical_not(is_me(peer)))
        def _():
            greet(peer)
    for peer in heads + final_to:
        count = count + 1 - b2i(is_me(peer))
    time_ref[...] = jnp.broadcast_to(
        jnp.transpose((jnp.broadcast_to(step_ref[...], (8, 64)).astype(F32) + 0.5) / NBINS)[:, 0:1], (64, 512)
    )
    load_noise.wait()
    pl.semaphore_wait(barrier, count)

    def first(g):
        return remote(noise_ref, buf.at[head_h, q_me], first_send.at[g], arrive.at[head_h, q_me], heads[g])

    for g in (0, 1):
        @pl.when(jnp.logical_not(is_me(heads[g])))
        def _():
            first(g).start()

        @pl.when(is_me(heads[g]))
        def _():
            pltpu.make_async_copy(noise_ref, buf.at[head_h, q_me], arrive.at[head_h, q_me]).start()

    load_data.wait()
    dsq_ref[...] = jnp.broadcast_to(
        jnp.sum(jnp.square(data_ref[...].astype(F32)), axis=1, keepdims=True), (256, 128)
    )

    def landed(h, q):
        pltpu.make_async_copy(noise_ref, buf.at[h, q], arrive.at[h, q]).wait()

    def hop(h, q, kind, peer):
        return remote(buf.at[h, q], buf.at[h, q], send.at[h, q, kind], arrive.at[h, q], peer)

    near = zi // 2

    def side(k):
        return near if k == 0 else 1 - near

    def around(h):
        return lax.rem(y - (2 * c + h) + 4, 4)

    def forwards(h, q, act):
        r = around(h)
        j, upward = q % 8, q < 8
        on_chain = r == 0

        inner = jnp.logical_or(zi == 1, zi == 2)

        @pl.when(on_chain & jnp.where(upward, inner, zi == 2))
        def _():
            act(hop(h, q, 0, zup))

        @pl.when(on_chain & jnp.where(upward, zi == 1, inner))
        def _():
            act(hop(h, q, 4, zdown))

        straight = jnp.where(upward == (near == 0), DIRECT[0], DIRECT[1])
        relay = jnp.logical_not(straight)

        @pl.when(jnp.logical_or(on_chain, jnp.logical_and(relay, jnp.logical_and(r == 1, j % 2 == 0))))
        def _():
            act(hop(h, q, 1, yup))

        @pl.when(jnp.logical_or(on_chain, jnp.logical_and(relay, jnp.logical_and(r == 3, j % 2 == 1))))
        def _():
            act(hop(h, q, 2, ydown))

        @pl.when(jnp.logical_and(on_chain, straight))
        def _():
            act(hop(h, q, 3, ypeers[1]))

    def waits_early(r, k):
        return jnp.logical_and(jnp.logical_or(r == 1, r == 3), not DIRECT[k])

    def tick(t, carry):
        for lagging in (0, 1):
            for h in (0, 1):
                r = around(h)
                s = t - LAG * lagging
                mine = r == 0
                if lagging == 1:
                    mine = jnp.logical_and(waits_early(r, 0), s < 8) | jnp.logical_and(waits_early(r, 1), s >= 8)

                @pl.when(jnp.logical_and(mine, jnp.logical_and(s >= 0, s < 16)))
                def _():
                    q = 8 * jnp.where(s < 8, near, 1 - near) + s % 8
                    landed(h, q)
                    forwards(h, q, lambda cp: cp.start())
        return carry

    def last_columns(k, lo, hi):
        def body(j, carry):
            for h in (0, 1):
                r = around(h)

                @pl.when(jnp.logical_not(jnp.logical_or(r == 0, waits_early(r, k))))
                def _():
                    landed(h, 8 * side(k) + j)
            return carry

        lax.fori_loop(lo, hi, body, 0)


    blocks = (4, 2, 2)
    offset = (0, 4, 6)
    base = (4 * near, 4 - 4 * near, 6 - 4 * near)

    def costs(k):
        def pair(b, carry):
            at = base[k] + 2 * b
            acc = jnp.concatenate([dsq_ref[...]] * 2, axis=1)
            sq = jnp.zeros((256, 128), F32)
            for h in (0, 1):
                piece = buf[h, pl.ds(2 * at, 4)].reshape(256, 512)
                acc -= 2.0 * lax.dot_general(
                    data_ref[:, 512 * h:512 * (h + 1)], piece, (((1,), (1,)), ((), ())), preferred_element_type=F32
                )
                for i in range(4):
                    wide = piece[:, 128 * i:128 * (i + 1)].astype(F32)
                    sq += wide * wide
            nsq = jnp.sum(jnp.transpose(sq), axis=0, keepdims=True)
            acc = (acc + nsq) * scale
            part[offset[k] + 2 * b] = acc[:, 0:128]
            part[offset[k] + 2 * b + 1] = acc[:, 128:256]
            return carry

        lax.fori_loop(0, blocks[k] // 2, pair, 0)

    def chunk(k):
        return pl.ds(offset[k], blocks[k])

    def core_sum(k):
        return remote(
            part.at[chunk(k), pl.ds(128 * (1 - c), 128)], half.at[chunk(k)], c_send.at[k], c_recv.at[k], other
        )

    def core_done(k):
        core_sum(k).wait()
        half[chunk(k)] = half[chunk(k)] + part[chunk(k), pl.ds(pl.multiple_of(128 * c, 128), 128)]

    def x_sum(k, i, slot):
        return remote(
            half.at[chunk(k), pl.ds(32 * xq(i), 32)], xin.at[slot, chunk(k)],
            x_send.at[k, i], x_recv.at[k, slot], xpeers[i - 1],
        )

    def x_start(k):
        for i in (1, 2, 3):
            x_sum(k, i, x).start()

    def z_sum(k):
        return remote(own.at[chunk(k)], zin.at[chunk(k)], z_send.at[k], z_recv.at[k], far)

    def x_done(k):
        acc = half[chunk(k), pl.ds(pl.multiple_of(32 * x, 32), 32)]
        for i in (1, 2, 3):
            x_sum(k, i, xq(i)).wait()
            acc += xin[xq(i), chunk(k)]
        own[chunk(k)] = acc
        z_sum(k).start()

    def slab(k, cc, xx):
        return s_ref.at[pl.ds(base[k], blocks[k]), pl.ds(128 * cc + 32 * xx, 32)]

    def z_done(k):
        z_sum(k).wait()
        mine = pl.ds(pl.multiple_of(128 * c + 32 * x, 32), 32)
        s_ref[pl.ds(base[k], blocks[k]), mine] = own[chunk(k)] + zin[chunk(k)]
        for i in (1, 2, 3):
            remote(slab(k, c, x), slab(k, c, x), gx_send.at[k, i], gx_recv.at[k, x], xpeers[i - 1]).start()

    def core_gather(k, cc):
        place = s_ref.at[pl.ds(base[k], blocks[k]), pl.ds(128 * cc, 128)]
        return remote(place, place, gc_send.at[k], gc_recv.at[k], other)

    def gx_done(k):
        for i in (1, 2, 3):
            remote(slab(k, c, x), slab(k, c, xq(i)), gx_send.at[k, i], gx_recv.at[k, xq(i)], xpeers[i - 1]).wait()
        core_gather(k, c).start()

    def gc_done(k):
        core_gather(k, c).wait_send()
        core_gather(k, 1 - c).wait_recv()

    srcc = y // 2

    def spread(act):
        for h in (0, 1):
            for cc in (0, 1):
                same = jnp.logical_and(c == cc, y == 2 * c + h)
                src = data_ref.at[:, pl.ds(512 * h, 512)]

                @pl.when(jnp.logical_not(same))
                def _():
                    peer = (zh * 8 + x * 2 + cc, zl * 4 + 2 * c + h)
                    act(remote(src, dt_ref.at[y], as_.at[h, cc], ar.at[y], peer), False)

                @pl.when(same)
                def _():
                    act(pltpu.make_async_copy(src, dt_ref.at[y], loc), True)

    lax.fori_loop(0, 8 + LAG, tick, 0)
    last_columns(0, 0, 8)
    costs(0)
    core_sum(0).start()
    lax.fori_loop(8 + LAG, 12 + LAG, tick, 0)
    core_done(0)
    x_start(0)
    last_columns(1, 0, 4)
    costs(1)
    core_sum(1).start()
    lax.fori_loop(12 + LAG, 16 + LAG, tick, 0)
    x_done(0)
    core_done(1)
    x_start(1)
    last_columns(1, 4, 8)
    costs(2)
    core_sum(2).start()
    x_done(1)
    core_done(2)
    x_start(2)
    spread(lambda cp, local: cp.start())
    x_done(2)
    z_done(0)
    gx_done(0)
    z_done(1)
    gx_done(1)
    z_done(2)
    gx_done(2)
    for k in range(3):
        gc_done(k)

    def lse0(v):
        m = jnp.max(v, axis=0)
        return m + jnp.log2(jnp.sum(jnp.exp2(v - m[None]), axis=0))

    def z_rows(k):
        for i, peer in enumerate(zpeers):
            remote(row.at[k], rz.at[k, zl], zs.at[k, i], zr.at[k, zl], peer).start()
        rz[k, zl] = row[k]

    def all_rows(k, total):
        for i, peer in enumerate(zpeers):
            remote(row.at[k], rz.at[k, zq(i + 1)], zs.at[k, i], zr.at[k, zq(i + 1)], peer).wait()
        ry[k, y] = total(rz[k])
        mine = ry.at[k, y]
        for i, peer in enumerate(ypeers):
            remote(mine, mine, ys.at[k, i], yr.at[k, y], peer).start()
        for i, peer in enumerate(ypeers):
            remote(mine, ry.at[k, yq(i + 1)], ys.at[k, i], yr.at[k, yq(i + 1)], peer).wait()
        return total(ry[k])

    for b in range(8):
        v = -s_ref[b]
        m = jnp.max(v, axis=0, keepdims=True)
        row[0, b:b + 1, :] = m + jnp.log2(jnp.sum(jnp.exp2(v - m), axis=0, keepdims=True))
    z_rows(0)
    f = -all_rows(0, lse0)
    fpot[...] = f
    m = f[0:1] - s_ref[0]
    for b in range(1, 8):
        m = jnp.maximum(m, f[b:b + 1] - s_ref[b])
    m = jnp.broadcast_to(jnp.max(m, axis=1, keepdims=True), (256, 128))
    tot = jnp.zeros((256, 128), F32)
    for b in range(8):
        tot += jnp.exp2(f[b:b + 1] - s_ref[b] - m)
    gpot[...] = -(m + jnp.log2(jnp.broadcast_to(jnp.sum(tot, axis=1, keepdims=True), (256, 128))))

    def add0(v):
        return jnp.sum(v, axis=0)

    def iteration(k, carry):
        g = gpot[...]
        f = fpot[...]
        for b in range(8):
            row[k, b:b + 1, :] = jnp.sum(jnp.exp2(g - s_ref[b] + f[b:b + 1]), axis=0, keepdims=True)
        z_rows(k)
        f = f - jnp.log2(all_rows(k, add0))
        fpot[...] = f
        tot = jnp.zeros((256, 128), F32)
        for b in range(8):
            tot += jnp.exp2(g - s_ref[b] + f[b:b + 1])
        gpot[...] = g - jnp.log2(jnp.broadcast_to(jnp.sum(tot, axis=1, keepdims=True), (256, 128)))
        return carry

    lax.fori_loop(1, ITERS, iteration, 0)

    def wsend(b, k, peer):
        return remote(w_ref.at[4 * c + b], wbuf.at[y, b], ws.at[k, b], wr.at[y, b], peer)

    def wpass(b, src, k, peer):
        return remote(wbuf.at[src, b], wbuf.at[src, b], ws.at[k, b], wr.at[src, b], peer)

    def wwait(b, src):
        remote(w_ref.at[b], wbuf.at[src, b], ws.at[0, b], wr.at[src, b], yup).wait_recv()

    left, right, opposite = yq(3), yq(1), yq(2)
    g = gpot[...]
    row[ITERS] = jnp.zeros((8, 128), F32)
    for b in range(4):
        e = jnp.exp2(g - s_ref[4 * c + b] + fpot[pl.ds(4 * c + b, 1), :])
        w_ref[4 * c + b] = e.astype(BF16)
        wsend(b, 0, yup).start()
        wsend(b, 1, ydown).start()
        wbuf[y, b] = e.astype(BF16)
        row[ITERS, b:b + 1, :] = jnp.sum(e, axis=0, keepdims=True)
    z_rows(ITERS)
    spread(lambda cp, local: cp.wait() if local else cp.wait_send())
    for k in range(4):
        @pl.when(jnp.logical_not(jnp.logical_and(srcc == c, y == k)))
        def _():
            peer = (zh * 8 + x * 2 + srcc, zl * 4 + k)
            remote(dt_ref.at[k], dt_ref.at[k], as_.at[0, 0], ar.at[k], peer).wait_recv()

    def wforward(b):
        if b % 2 == 0:
            wwait(b, left)
            wpass(b, left, 2, yup).start()
        else:
            wwait(b, right)
            wpass(b, right, 2, ydown).start()

    def quad(i):
        return (n, (4 * zg + (zi + i) % 4) * 4 + y)

    def quad_sum(h, i, slot):
        return remote(stage.at[h, (zi + i) % 4], qin.at[h, slot], qs.at[h, i], qr.at[h, slot], quad(i))

    def mul(b, k):
        prod = lax.dot_general(wbuf[k, b], dt_ref[k], (((0,), (0,)), ((), ())), preferred_element_type=F32)
        return prod.reshape(2, 64, 512)

    def place(b):
        return b // 2, pl.ds(2 * (b % 2), 2)

    def add(b, k):
        h, at = place(b)
        tpart[h, at] += mul(b, k)

    def finish(b):
        wwait(b, opposite)
        h, at = place(b)
        acc = tpart[h, at] + mul(b, opposite)
        tpart[h, at] = acc
        stage[h, at] = acc.astype(BF16)

    def quad_start(h):
        for i in (1, 2, 3):
            quad_sum(h, i, zi).start()

    for b in range(4):
        h, at = place(b)
        tpart[h, at] = mul(b, y)
    wforward(0)
    wforward(1)
    add(0, left)
    add(1, right)
    wforward(2)
    wforward(3)
    wwait(0, right)
    add(0, right)
    wwait(1, left)
    add(1, left)
    finish(0)
    finish(1)
    quad_start(0)
    add(2, left)
    add(3, right)
    wwait(2, right)
    add(2, right)
    wwait(3, left)
    add(3, left)
    finish(2)
    finish(3)
    quad_start(1)

    def final(h):
        return remote(fin.at[h], got.at[zg], fs.at[h], fr.at[zg], final_to[h])

    for h in (0, 1):
        acc = tpart[h, zi]
        for i in (1, 2, 3):
            quad_sum(h, i, (zi + i) % 4).wait()
            acc += qin[h, (zi + i) % 4].astype(F32)
        fin[h] = acc.astype(BF16)

        @pl.when(jnp.logical_not(is_me(final_to[h])))
        def _():
            final(h).start()

        @pl.when(is_me(final_to[h]))
        def _():
            pltpu.make_async_copy(fin.at[h], got.at[zg], fr.at[zg]).start()

    total = 1.0 / all_rows(ITERS, add0)
    columns = jnp.transpose(total)
    mine_b = 2 * zh + x // 2
    picked = jnp.zeros((128, 1), F32)
    for b in range(4):
        picked = jnp.where(mine_b == b, columns[:, b:b + 1], picked)
    picked = jnp.where(x % 2 == 0, picked[0:64], picked[64:128])

    for g in (0, 1):
        @pl.when(jnp.logical_not(is_me(heads[g])))
        def _():
            first(g).wait_send()

    def drain(q, carry):
        for h in (0, 1):
            forwards(h, q, lambda cp: cp.wait_send())
        return carry

    lax.fori_loop(0, 16, drain, 0)
    for b in range(4):
        wsend(b, 0, yup).wait_send()
        wsend(b, 1, ydown).wait_send()
        if b % 2 == 0:
            wpass(b, left, 2, yup).wait_send()
        else:
            wpass(b, right, 2, ydown).wait_send()
    for g in (0, 1):
        pltpu.make_async_copy(fin.at[0], got.at[g], fr.at[g]).wait()
    out_ref[...] = (got[0].astype(F32) + got[1].astype(F32)) * picked
    for h in (0, 1):
        @pl.when(jnp.logical_not(is_me(final_to[h])))
        def _():
            final(h).wait_send()


DMA = pltpu.SemaphoreType.DMA


def fused_call(noise, data, timestep):
    scale = LOG2E / (16384.0 * EPS)
    rounds = ITERS + 1
    return pl.pallas_call(
        functools.partial(fused_kernel, scale),
        out_shape=[jax.ShapeDtypeStruct((64, 512), F32), jax.ShapeDtypeStruct((64, 512), F32)],
        in_specs=[pl.BlockSpec(memory_space=pl.ANY)] * 2 + [pl.BlockSpec(memory_space=VMEM)],
        out_specs=[pl.BlockSpec(memory_space=VMEM)] * 2,
        scratch_shapes=[
            VMEM((64, 512), BF16), VMEM((256, 1024), BF16), VMEM((256, 128), F32),
            VMEM((2, 16, 64, 512), BF16),
            VMEM((8, 256, 128), F32), VMEM((8, 128, 128), F32), VMEM((4, 8, 32, 128), F32),
            VMEM((8, 32, 128), F32), VMEM((8, 32, 128), F32), VMEM((8, 256, 128), F32),
            VMEM((256, 128), F32), VMEM((8, 128), F32), VMEM((rounds, 8, 128), F32), VMEM((rounds, 8, 8, 128), F32),
            VMEM((rounds, 4, 8, 128), F32),
            VMEM((8, 256, 128), BF16), VMEM((4, 256, 512), BF16), VMEM((4, 4, 256, 128), BF16),
            VMEM((2, 4, 64, 512), F32), VMEM((2, 4, 64, 512), BF16), VMEM((2, 4, 64, 512), BF16),
            VMEM((2, 64, 512), BF16), VMEM((2, 64, 512), BF16),
            DMA((2,)), DMA((2,)), DMA((2, 16)), DMA((2, 16, 5)),
            DMA((3,)), DMA((3,)), DMA((3, 4)), DMA((3, 4)), DMA((3,)), DMA((3,)),
            DMA((3, 4)), DMA((3, 4)), DMA((3,)), DMA((3,)),
            DMA((rounds, 7)), DMA((rounds, 8)), DMA((rounds, 3)), DMA((rounds, 4)),
            DMA((2, 2)), DMA((4,)), DMA, DMA((3, 4)), DMA((4, 4)),
            DMA((2, 4)), DMA((2, 4)), DMA((2,)), DMA((2,)),
        ],
        compiler_params=pltpu.CompilerParams(
            collective_id=1, has_side_effects=True, vmem_limit_bytes=62 * 1024 * 1024
        ),
    )(noise, data, timestep)


def per_device(noise, data, timestep):
    targets, t_wide = fused_call(noise, data, timestep.reshape(1, 64))
    noise_f = noise.astype(F32)
    t_val = t_wide
    inputs_t = ((1.0 - t_val) * noise_f + t_val * targets).astype(BF16)
    velocity = (targets - noise_f).astype(BF16)
    return (inputs_t, velocity)


def solution(mesh):
    placed = (P("noise", "dp"), P("dp", "noise"), P("noise"))
    return jax.shard_map(
        per_device,
        mesh=mesh,
        in_specs=placed,
        out_specs=(P("noise", "dp"), P("noise", "dp")),
        check_vma=False,
    )
```
